512 devices in a mesh: arm: 8 (over x_lo, y), sx: 32 (over z, core), sy: 2 (over x_hi).
Axes of the slice: x: 4 (x_hi: 2, x_lo: 2; x = x_hi * 2 + x_lo), y: 4, z: 16, core: 2. Of those that a mesh axis runs over, the one named last changes fastest.
Arguments:
- forward_end: float32 [16, 128, 256, 256], P('arm', 'sx', 'sy'), may hold values from 0.5 to 2
- partner_end: float32 [16, 128, 256, 256], P('arm', 'sx', 'sy'), may hold values from 0.5 to 2
- potential: float32 [2, 128, 256, 256], P(None, 'sx', 'sy'), may hold values from -3 to 3
- species_label: int32 [16], P('arm'), may hold values from 0 to 1
- arm_length: int32 [16], P('arm'), may hold values from 1 to 3, as said below
Outputs:
- conjugate: float32 [16, 128, 256, 256], P('arm', 'sx', 'sy')
- density: float32 [2, 128, 256, 256], P(None, 'sx', 'sy')
The draws below stay inside these ranges and needn't reach their ends.
Inputs may be any that keep to these rules, and one draw needn't show every extreme that they name: `arm_length`: some arm has exactly 3 steps in every draw.
All inputs are finite; a program needn't handle non-finite values.
Results may differ from the reference program's by a relative error of at most 0.000036.
Values sent between devices are 32-bit elements; how exact they have to be, the bound alone decides.
A program may use at most 64 MiB of HBM per device.

```python
import math
import jax
import jax.numpy as jnp

ARMS = 16
SPECIES = 2
MAXSTEPS = 3
CZ = 256
NX = 128
NY = 256


def draw_arm_length(key, part):
    key = jax.random.fold_in(key, 7)
    first, second = jax.random.split(key)
    base = jax.random.randint(first, (ARMS,), 1, MAXSTEPS + 1)
    chosen = jax.random.randint(second, (), 0, ARMS)
    return jnp.where(jnp.arange(ARMS) == chosen, MAXSTEPS, base).astype(jnp.int32)


def set_ends(entries, stream_key, low, high):
    dims = entries.shape
    index_at = [jax.random.randint(jax.random.fold_in(stream_key, axis), (), 0, dims[axis]) for axis in range(len(dims))]
    entries = entries.at[tuple(index_at)].set(low)
    longest = dims.index(max(dims))
    index_at[longest] = (index_at[longest] + 1) % dims[longest]
    return entries.at[tuple(index_at)].set(high)


def steps_of(own_key, shape, cuts, smallest, high):
    level, own = 1.0, jax.random.fold_in(own_key, 6)
    for axis_at, parts in cuts:
        draws = jnp.exp(jax.random.uniform(jax.random.fold_in(own, axis_at), (parts,), jnp.float32, smallest / len(cuts), high / len(cuts)))
        level = level * jnp.repeat(draws, shape[axis_at] // parts).reshape([-1 if axis == axis_at else 1 for axis in range(len(shape))])
    return level


def gaussian(stream_key, shape, spread, most, cuts=(), held_as=jnp.bfloat16):
    values = jax.random.normal(stream_key, shape, jnp.float32) * spread
    if len(cuts) > 0:
        values = steps_of(stream_key, shape, cuts, -0.22, 0.18) * values
    return jnp.clip(values, min=-most, max=most).astype(held_as)


def setup_inputs(seed: int = 0) -> dict:
    seeds = jax.random.split(jax.random.key(seed), 6)
    return {
        "forward_end": jnp.clip(jnp.exp(math.log(2.0) - 1.3862944 * jax.random.uniform(seeds[0], (ARMS, NX, NY, CZ), jnp.float32) ** steps_of(seeds[0], (ARMS, NX, NY, CZ), ((0, 8), (1, 32), (2, 2)), -0.2, 0.2)), 0.5, 2.0),
        "partner_end": jnp.clip(jnp.exp(math.log(2.0) - 1.3862944 * jax.random.uniform(seeds[1], (ARMS, NX, NY, CZ), jnp.float32) ** steps_of(seeds[1], (ARMS, NX, NY, CZ), ((0, 8), (1, 32), (2, 2)), -0.2, 0.2)), 0.5, 2.0),
        "potential": gaussian(seeds[2], (SPECIES, NX, NY, CZ), 0.5, 3.0, ((1, 32), (2, 2)), jnp.float32),
        "species_label": set_ends(jax.random.randint(seeds[3], (ARMS,), 0, 2), jax.random.fold_in(seeds[3], 1), 0, 1).astype(jnp.int32),
        "arm_length": draw_arm_length(jax.random.fold_in(seeds[5], 71), 0),
    }


STIFF = 0.16


def one_step(field, factor):
    inner = factor * field
    laplace = -6.0 * inner
    for axis_num in (1, 2, 3):
        laplace = laplace + jnp.roll(inner, 1, axis_num) + jnp.roll(inner, -1, axis_num)
    return factor * (inner + STIFF * laplace)


def reference(forward_end, partner_end, potential, species_label, arm_length):
    logs = jnp.log(forward_end)
    logsum = jnp.sum(logs, axis=0)
    current = jnp.exp(logsum[None] - logs)
    factor = jnp.exp(-0.5 * jnp.where((species_label == 1)[:, None, None, None], potential[1][None], potential[0][None]))
    for step_index in range(MAXSTEPS):
        updated = one_step(current, factor)
        active = (arm_length > step_index)[:, None, None, None]
        current = jnp.where(active, updated, current)
    product = partner_end * current
    dens_zero = jnp.sum(jnp.where((species_label == 0)[:, None, None, None], product, 0.0), axis=0)
    dens_one = jnp.sum(jnp.where((species_label == 1)[:, None, None, None], product, 0.0), axis=0)
    return current, jnp.stack([dens_zero, dens_one])
```

```python
import jax
import jax.numpy as jnp
from jax import lax
from jax.experimental import pallas as pl
from jax.experimental.pallas import tpu as pltpu
from jax.sharding import PartitionSpec as P

MESH = pl.DeviceIdType.MESH
F32 = jnp.float32
ROWS, NYL, LANES = 4, 128, 128
YD, Y0 = 160, 16
BLK = 24


def kernel(
    lab, length, fwd, par, pot, conj, dens,
    fv, pv, uv, p, prx, pext, c, ifac, va, vb, cj, dp, drx, do,
    lsem, bsend, brecv, psend, precv, hsend, hrecv, dsend, drecv,
):
    arm, sx, sy = lax.axis_index("arm"), lax.axis_index("sx"), lax.axis_index("sy")
    x, y = arm // 4, arm % 4
    xs = [x, 1 - x]
    ys = [y, y + 1 - 2 * (y % 2), (y + 2) % 4, 3 - y]
    peers = [(xs[d // 4], ys[d % 4]) for d in range(8)]
    up, down, other = (sx + 1) % 32, (sx + 31) % 32, 1 - sy

    def arm_dev(d):
        return {"arm": peers[d][0] * 4 + peers[d][1]}

    around = [{"sx": up}, {"sx": down}, {"sy": other}, {"sx": up, "sy": other}, {"sx": down, "sy": other}]

    loads = []

    def load(src, dst):
        cp = pltpu.make_async_copy(src, dst, lsem.at[len(loads)])
        cp.start()
        loads.append(cp)

    for src, dst in ((fwd, fv), (pot, uv), (par, pv)):
        for h in range(2):
            load(src.at[:, :, :, pl.ds(h * LANES, LANES)], dst.at[:, :, h])

    barrier = pltpu.get_barrier_semaphore()
    for d in range(1, 8):
        pl.semaphore_signal(barrier, inc=1, device_id=arm_dev(d), device_id_type=MESH)
    for dev in around:
        pl.semaphore_signal(barrier, inc=1, device_id=dev, device_id_type=MESH)

    loads[0].wait()
    loads[1].wait()

    @pl.loop(0, ROWS)
    def _(r):
        for h in range(2):
            p[r, h] = fv[0, r, h] * fv[1, r, h]

    pl.semaphore_wait(barrier, 12)

    def send(src, dst, ssem, rsem, dev):
        cp = pltpu.make_async_remote_copy(
            src_ref=src, dst_ref=dst, send_sem=ssem, recv_sem=rsem, device_id=dev, device_id_type=MESH
        )
        cp.start()
        return cp

    sent = []
    rs = []
    for d in range(1, 8):
        px, py = peers[d]
        rs.append(send(p.at[py, px], prx.at[d], psend.at[d], precv.at[d], arm_dev(d)))
    sent += rs

    loads[2].wait()
    loads[3].wait()
    l = [lab[a] == 1 for a in range(2)]

    @pl.loop(0, ROWS)
    def _(r):
        for h in range(2):
            for b in range(0, NYL, 32):
                u0, u1 = uv[0, r, h, b:b + 32], uv[1, r, h, b:b + 32]
                for a in range(2):
                    e = jnp.exp(-0.5 * jnp.where(l[a], u1, u0))
                    inv = 1.0 / e
                    c[a, r + 3, h, Y0 + b:Y0 + b + 32] = e / fv[a, r, h, b:b + 32]
                    c[2 + a, r + 3, h, Y0 + b:Y0 + b + 32] = (0.16 * e) * e
                    ifac[a, r, h, b:b + 32] = inv

    own = pl.ds(Y0, NYL)
    lo_in, lo_out = pl.ds(Y0, 8), pl.ds(Y0 - 8, 8)
    hi_in, hi_out = pl.ds(Y0 + NYL - 8, 8), pl.ds(Y0 + NYL, 8)
    UPS = (pl.ds(4, 3), pl.ds(0, 3))
    DNS = (pl.ds(3, 3), pl.ds(7, 3))
    OWN = (pl.ds(3, 4), pl.ds(3, 4))

    def halo(buf, first, ss, rs_):
        out = []
        k = first
        for dev, rows in ((around[2], OWN), (around[3], UPS), (around[4], DNS)):
            for a, b in ((lo_in, hi_out), (hi_in, lo_out)):
                out.append(send(buf(rows[0], a), buf(rows[1], b), ss.at[k], rs_.at[k], dev))
                k += 1
        return out

    coef = []
    coef.append(send(c.at[pl.ds(0, 2), UPS[0], :, own], c.at[pl.ds(0, 2), UPS[1], :, own], hsend.at[0], hrecv.at[0], around[0]))
    coef.append(send(c.at[pl.ds(0, 2), DNS[0], :, own], c.at[pl.ds(0, 2), DNS[1], :, own], hsend.at[1], hrecv.at[1], around[1]))
    coef.append(send(c.at[pl.ds(2, 2), pl.ds(5, 2), :, own], c.at[pl.ds(2, 2), pl.ds(1, 2), :, own], hsend.at[2], hrecv.at[2], around[0]))
    coef.append(send(c.at[pl.ds(2, 2), pl.ds(3, 2), :, own], c.at[pl.ds(2, 2), pl.ds(7, 2), :, own], hsend.at[3], hrecv.at[3], around[1]))
    coef += halo(lambda r_, y_: c.at[:, r_, :, y_], 4, hsend, hrecv)
    sent += coef

    for cp in rs:
        cp.wait_recv()
    for b in range(0, NYL, 32):
        acc = p[y, x, b:b + 32]
        for d in range(1, 8):
            acc = acc * prx[d, b:b + 32]
        pext[3 + y, x, Y0 + b:Y0 + b + 32] = acc
    ag = []
    mine = pext.at[3 + y, x, own]
    for d in range(1, 8):
        ag.append(send(mine, mine, psend.at[8 + d], precv.at[8 + d], arm_dev(d)))
    sent += ag
    for cp in ag:
        cp.wait_recv()

    ph = []
    ph.append(send(pext.at[UPS[0], :, own], pext.at[UPS[1], :, own], hsend.at[10], hrecv.at[10], around[0]))
    ph.append(send(pext.at[DNS[0], :, own], pext.at[DNS[1], :, own], hsend.at[11], hrecv.at[11], around[1]))
    ph += halo(lambda r_, y_: pext.at[r_, :, y_], 12, hsend, hrecv)
    sent += ph

    for cp in coef:
        cp.wait_recv()
    for cp in ph:
        cp.wait_recv()

    @pl.loop(0, 10)
    def _(r):
        for h in range(2):
            for b in range(8, 152, BLK):
                q = pext[r, h, b:b + BLK]
                for a in range(2):
                    va[a, r, h, b:b + BLK] = q * c[a, r, h, b:b + BLK]

    lane = lax.broadcasted_iota(jnp.int32, (BLK, LANES), 1)

    def advance(src, a, r, b, n, active):
        first, last = lane[:n] == 0, lane[:n] == LANES - 1
        v = [src[a, r, h, b:b + n] for h in range(2)]
        fwd_ = [pltpu.roll(t, 1, 1) for t in v]
        bwd = [pltpu.roll(t, LANES - 1, 1) for t in v]
        out = []
        for h in range(2):
            s = src[a, r - 1, h, b:b + n] + src[a, r + 1, h, b:b + n]
            s = s + (src[a, r, h, b - 1:b + n - 1] + src[a, r, h, b + 1:b + n + 1])
            s = s + (jnp.where(first, fwd_[1 - h], fwd_[h]) + jnp.where(last, bwd[1 - h], bwd[h]))
            new = c[2 + a, r, h, b:b + n] * (0.25 * v[h] + s)
            out.append(jnp.where(active, new, v[h]))
        return out

    for t, (src, dst) in enumerate(((va, vb), (vb, va))):
        for a in range(2):
            active = length[a] > t

            @pl.loop(1 + t, 9 - t)
            def _(r):
                for b in range(8, 152, BLK):
                    out = advance(src, a, r, b, BLK, active)
                    for h in range(2):
                        dst[a, r, h, b:b + BLK] = out[h]

    loads[4].wait()
    loads[5].wait()
    ds_ = []
    for i in range(1, 5):
        r = ys[i % 4]
        for b in range(0, NYL, 16):
            w = []
            for a in range(2):
                out = advance(va, a, r + 3, Y0 + b, 16, length[a] > 2)
                ws = []
                for h in range(2):
                    q = out[h] * ifac[a, r, h, b:b + 16]
                    cj[a, r, h, b:b + 16] = q
                    ws.append(q * pv[a, r, h, b:b + 16])
                w.append(ws)
            for h in range(2):
                one = jnp.where(l[0], w[0][h], 0.0) + jnp.where(l[1], w[1][h], 0.0)
                zero = jnp.where(l[0], 0.0, w[0][h]) + jnp.where(l[1], 0.0, w[1][h])
                dp[0, r, h, b:b + 16] = zero
                dp[1, r, h, b:b + 16] = one
        for j in (i % 4, i % 4 + 4):
            if j:
                px, py = peers[j]
                ds_.append(send(dp.at[px, py], drx.at[j], dsend.at[j], drecv.at[j], arm_dev(j)))
    sent += ds_
    stores = []
    for h in range(2):
        cp = pltpu.make_async_copy(cj.at[:, :, h], conj.at[:, :, :, pl.ds(h * LANES, LANES)], lsem.at[6 + h])
        cp.start()
        stores.append(cp)
    for cp in ds_:
        cp.wait_recv()
    for h in range(2):
        for b in range(0, NYL, 32):
            acc = dp[x, y, h, b:b + 32]
            for d in range(1, 8):
                acc = acc + drx[d, h, b:b + 32]
            do[x, y, h, b:b + 32] = acc
    dg = []
    piece = do.at[x, y]
    for d in range(1, 8):
        dg.append(send(piece, piece, dsend.at[8 + d], drecv.at[8 + d], arm_dev(d)))
    sent += dg
    for cp in dg:
        cp.wait_recv()
    for h in range(2):
        cp = pltpu.make_async_copy(do.at[:, :, h], dens.at[:, :, :, pl.ds(h * LANES, LANES)], lsem.at[8 + h])
        cp.start()
        stores.append(cp)
    for cp in sent:
        cp.wait_send()
    for cp in stores:
        cp.wait()


def local(forward_end, partner_end, potential, species_label, arm_length):
    full = (2, ROWS, 2, NYL, LANES)
    ext = (10, 2, YD, LANES)
    dma = pltpu.SemaphoreType.DMA
    return pl.pallas_call(
        kernel,
        name="star",
        out_shape=[jax.ShapeDtypeStruct(forward_end.shape, F32), jax.ShapeDtypeStruct(potential.shape, F32)],
        in_specs=[pl.BlockSpec(memory_space=pltpu.SMEM)] * 2 + [pl.BlockSpec(memory_space=pl.ANY)] * 3,
        out_specs=[pl.BlockSpec(memory_space=pl.ANY)] * 2,
        scratch_shapes=[
            pltpu.VMEM(full, F32), pltpu.VMEM(full, F32), pltpu.VMEM(full, F32),
            pltpu.VMEM((ROWS, 2, NYL, LANES), F32), pltpu.VMEM((8, NYL, LANES), F32),
            pltpu.VMEM(ext, F32), pltpu.VMEM((4,) + ext, F32), pltpu.VMEM(full, F32),
            pltpu.VMEM((2,) + ext, F32), pltpu.VMEM((2,) + ext, F32), pltpu.VMEM(full, F32),
            pltpu.VMEM(full, F32), pltpu.VMEM((8, 2, NYL, LANES), F32), pltpu.VMEM(full, F32),
            dma((10,)), dma((1,)), dma((1,)), dma((16,)), dma((16,)), dma((18,)), dma((18,)), dma((16,)), dma((16,)),
        ],
        compiler_params=pltpu.CompilerParams(collective_id=0, has_side_effects=True, vmem_limit_bytes=50 << 20),
        cost_estimate=pl.CostEstimate(flops=20_000_000, bytes_accessed=5 << 20, transcendentals=1 << 19),
    )(species_label, arm_length, forward_end, partner_end, potential)


def solution(mesh):
    return jax.shard_map(
        local,
        mesh=mesh,
        in_specs=(
            P("arm", "sx", "sy", None),
            P("arm", "sx", "sy", None),
            P(None, "sx", "sy", None),
            P("arm"),
            P("arm"),
        ),
        out_specs=(P("arm", "sx", "sy", None), P(None, "sx", "sy", None)),
        check_vma=False,
    )
```

```python
import jax
import jax.numpy as jnp
from jax import lax
from jax.experimental import pallas as pl
from jax.experimental.pallas import tpu as pltpu
from jax.sharding import PartitionSpec as P

MESH = pl.DeviceIdType.MESH
F32 = jnp.float32
ROWS, NYL, LANES = 4, 128, 128
YD, Y0 = 160, 16
SEG = (((0, 24, 80),), ((0, 104, 24), (24, 0, 24)))
YC = (80, 48)
DSEG = (((0, 32, 64),), ((0, 96, 32), (32, 0, 32)))
TILES = (tuple(range(3, 13)), (12, 13, 14, 15, 16, -1, 0, 1, 2, 3))
LAST = (tuple(range(4, 12)), (12, 13, 14, 15, 0, 1, 2, 3))


def kernel(
    lab_h, len_h, fwd, par, pot, conj, dens,
    lab, length, fv, pv, uv, p0, p1, prx0, prx1, pf0, pf1, g0, g1, q0, q1, ifac,
    es, ce, pes, pe, gp, v1, v2, v3, dp, drx,
    lsem, psend, precv, hsend, hrecv, dsend, drecv,
):
    arm, sx, sy = lax.axis_index("arm"), lax.axis_index("sx"), lax.axis_index("sy")
    x, y = arm // 4, arm % 4
    xs = [x, 1 - x]
    ys = [y, y + 1 - 2 * (y % 2), (y + 2) % 4, 3 - y]
    peers = [(xs[d // 4], ys[d % 4]) for d in range(8)]
    up, down, other = (sx + 1) % 32, (sx + 31) % 32, 1 - sy
    p, prx, pf, g, q = (p0, p1), (prx0, prx1), (pf0, pf1), (g0, g1), (q0, q1)

    def arm_dev(d):
        return {"arm": peers[d][0] * 4 + peers[d][1]}

    around = [{"sx": up}, {"sx": down}, {"sy": other}, {"sx": up, "sy": other}, {"sx": down, "sy": other}]

    loads = []
    for src, dst in ((fwd, fv), (pot, uv), (lab_h, lab), (len_h, length), (par, pv)):
        cp = pltpu.make_async_copy(src, dst, lsem.at[len(loads)])
        cp.start()
        loads.append(cp)
    stores = []
    sent = []

    def send(src, dst, ssem, rsem, k, dev):
        cp = pltpu.make_async_remote_copy(
            src_ref=src, dst_ref=dst, send_sem=ssem.at[k], recv_sem=rsem.at[k], device_id=dev, device_id_type=MESH
        )
        cp.start()
        sent.append(cp)
        return cp

    barrier = pltpu.get_barrier_semaphore()
    for d in range(1, 8):
        pl.semaphore_signal(barrier, inc=1, device_id=arm_dev(d), device_id_type=MESH)
    for dev in around:
        pl.semaphore_signal(barrier, inc=1, device_id=dev, device_id_type=MESH)

    loads[0].wait()

    def lanes(h):
        return slice(h * LANES, (h + 1) * LANES)

    @pl.loop(0, ROWS)
    def _(r):
        for k in range(2):
            for o, s, n in SEG[k]:
                for h in range(2):
                    p[k][r, h, o:o + n] = fv[0, r, s:s + n, lanes(h)] * fv[1, r, s:s + n, lanes(h)]

    pl.semaphore_wait(barrier, 12)


    rs = [[], []]
    for k in range(2):
        for d in range(1, 8):
            px, py = peers[d]
            rs[k].append(send(p[k].at[py, px], prx[k].at[d], psend, precv, 16 * k + d, arm_dev(d)))


    for i in (1, 2, 3):
        loads[i].wait()
    l = [lab[a] == 1 for a in range(2)]

    g_rows = ((pl.ds(4, 3), pl.ds(0, 3)), (pl.ds(3, 3), pl.ds(7, 3)))
    q_rows = ((pl.ds(5, 2), pl.ds(1, 2)), (pl.ds(3, 2), pl.ds(7, 2)))
    coef = [[], []]
    for k in range(2):

        @pl.loop(0, ROWS)
        def _(r):
            for o, s, n in SEG[k]:
                for h in range(2):
                    for b in range(0, n, 8):
                        ya, oa = s + b, o + b
                        u0, u1 = (uv[i, r, ya:ya + 8, lanes(h)] for i in range(2))
                        for a in range(2):
                            e = jnp.exp(-0.5 * jnp.where(l[a], u1, u0))
                            ge = e / fv[a, r, ya:ya + 8, lanes(h)]
                            qe = (0.16 * e) * e
                            g[k][r + 3, a, h, oa:oa + 8] = ge
                            q[k][r + 3, a, h, oa:oa + 8] = qe
                            ifac[a, r, ya:ya + 8, lanes(h)] = 1.0 / e
                            i, j = a * 6 + h * 3, 12 + a * 4 + h * 2
                            if ya == 0:
                                es[0, r, i:i + 3] = ge[0:3]
                                es[0, r, j:j + 2] = qe[0:2]
                            if ya == NYL - 8:
                                es[1, r, i:i + 3] = ge[5:8]
                                es[1, r, j:j + 2] = qe[6:8]

        for i in range(2):
            coef[k].append(send(g[k].at[g_rows[i][0]], g[k].at[g_rows[i][1]], hsend, hrecv, 4 * k + i, around[i]))
            coef[k].append(send(q[k].at[q_rows[i][0]], q[k].at[q_rows[i][1]], hsend, hrecv, 4 * k + 2 + i, around[i]))

    def edges(src, dst, first):
        out = []
        for dev, rows, to in ((2, pl.ds(0, 4), pl.ds(3, 4)), (3, pl.ds(1, 3), pl.ds(0, 3)), (4, pl.ds(0, 3), pl.ds(7, 3))):
            for side in range(2):
                out.append(send(src.at[side, rows], dst.at[side, to], hsend, hrecv, first + len(out), around[dev]))
        return out

    coef[1] += edges(es, ce, 8)


    ag = [[], []]
    for k in range(2):
        for cp in rs[k]:
            cp.wait_recv()
        for b in range(0, YC[k], 16):
            acc = p[k][y, x, b:b + 16]
            for d in range(1, 8):
                acc = acc * prx[k][d, b:b + 16]
            pf[k][3 + y, x, b:b + 16] = acc
        mine = pf[k].at[3 + y, x]
        for d in range(1, 8):
            ag[k].append(send(mine, mine, psend, precv, 16 * k + 8 + d, arm_dev(d)))


    ph = [[], []]
    for k in range(2):
        for cp in ag[k]:
            cp.wait_recv()
        for i in range(2):
            ph[k].append(send(pf[k].at[g_rows[i][0]], pf[k].at[g_rows[i][1]], hsend, hrecv, 14 + 2 * k + i, around[i]))
        if k == 1:
            for r in range(ROWS):
                for h in range(2):
                    pes[0, r, 3 * h:3 * h + 3] = pf1[r + 3, h, 24:27]
                    pes[1, r, 3 * h:3 * h + 3] = pf1[r + 3, h, 21:24]
            ph[1] += edges(pes, pe, 18)


    lane = lax.broadcasted_iota(jnp.int32, (8, LANES), 1)
    first, last = lane == 0, lane == LANES - 1

    def q_tile(a, r, h, t):
        if t in (-1, 16):
            return gp[0 if t == 16 else 1, r, a, h]
        if 3 <= t < 13:
            return q0[r, a, h, 8 * t - 24:8 * t - 16]
        o = 8 * t - 104 if t >= 13 else 8 * t + 24
        return q1[r, a, h, o:o + 8]

    def advance(src, a, r, t, active):
        b = Y0 + 8 * t
        v = [src[a, r, h, b:b + 8] for h in range(2)]
        right = [pltpu.roll(w, 1, 1) for w in v]
        left = [pltpu.roll(w, LANES - 1, 1) for w in v]
        out = []
        for h in range(2):
            s = src[a, r - 1, h, b:b + 8] + src[a, r + 1, h, b:b + 8]
            s = s + (src[a, r, h, b - 1:b + 7] + src[a, r, h, b + 1:b + 9])
            s = s + (jnp.where(first, right[1 - h], right[h]) + jnp.where(last, left[1 - h], left[h]))
            new = q_tile(a, r, h, t) * (0.25 * v[h] + s)
            out.append(jnp.where(active, new, v[h]))
        return out

    loads[4].wait()
    drs = [[], []]
    for k in range(2):
        for cp in coef[k]:
            cp.wait_recv()
        for cp in ph[k]:
            cp.wait_recv()

        @pl.loop(0, 10)
        def _(r):
            for o, s, n in SEG[k]:
                for h in range(2):
                    f = pf[k][r, h, o:o + n]
                    for a in range(2):
                        v1[a, r, h, Y0 + s:Y0 + s + n] = f * g[k][r, a, h, o:o + n]
            if k == 1:
                for side, b in ((0, Y0 + NYL), (1, Y0 - 3)):
                    for h in range(2):
                        f = pe[side, r, 3 * h:3 * h + 3]
                        for a in range(2):
                            i, j = a * 6 + h * 3, 12 + a * 4 + h * 2
                            v1[a, r, h, b:b + 3] = f * ce[side, r, i:i + 3]
                            gp[side, r, a, h, 6 * side:6 * side + 2] = ce[side, r, j:j + 2]

        for t, (src, dst) in enumerate(((v1, v2), (v2, v3))):
            act = [length[a] > t for a in range(2)]

            @pl.loop(1 + t, 9 - t)
            def _(r):
                for tile in TILES[k]:
                    b = Y0 + 8 * tile
                    for a in range(2):
                        out = advance(src, a, r, tile, act[a])
                        for h in range(2):
                            dst[a, r, h, b:b + 8] = out[h]

        act = [length[a] > 2 for a in range(2)]
        for i in (1, 2, 3, 0):
            r = ys[i]
            for n, tile in enumerate(LAST[k]):
                b = 8 * tile
                w = []
                for a in range(2):
                    out = advance(v3, a, r + 3, tile, act[a])
                    ws = []
                    for h in range(2):
                        c = out[h] * ifac[a, r, b:b + 8, lanes(h)]
                        conj[a, r, b:b + 8, lanes(h)] = c
                        ws.append(c * pv[a, r, b:b + 8, lanes(h)])
                    w.append(ws)
                for h in range(2):
                    dp[k, 0, r, 8 * n:8 * n + 8, lanes(h)] = jnp.where(l[0], 0.0, w[0][h]) + jnp.where(l[1], 0.0, w[1][h])
                    dp[k, 1, r, 8 * n:8 * n + 8, lanes(h)] = jnp.where(l[0], w[0][h], 0.0) + jnp.where(l[1], w[1][h], 0.0)
            for j in (i, i + 4):
                if j:
                    px, py = peers[j]
                    drs[k].append(send(dp.at[k, px, py], drx.at[k, j], dsend, drecv, 24 * k + j, arm_dev(j)))


    dag = []
    for k in range(2):
        for cp in drs[k]:
            cp.wait_recv()
        for m, (o, s, n) in enumerate(DSEG[k]):
            for h in range(2):
                for b in range(0, n, 16):
                    acc = dp[k, x, y, o + b:o + b + 16, lanes(h)]
                    for d in range(1, 8):
                        acc = acc + drx[k, d, o + b:o + b + 16, lanes(h)]
                    dens[x, y, s + b:s + b + 16, lanes(h)] = acc
            piece = dens.at[x, y, pl.ds(s, n)]
            for d in range(1, 8):
                dag.append(send(piece, piece, dsend, drecv, 24 * k + 8 * (m + 1) + d, arm_dev(d)))

    for cp in dag:
        cp.wait_recv()
    for cp in sent:
        cp.wait_send()


def local(forward_end, partner_end, potential, species_label, arm_length):
    full = pltpu.VMEM((2, ROWS, NYL, 2 * LANES), F32)
    dma = pltpu.SemaphoreType.DMA

    def v(*shape):
        return pltpu.VMEM(shape, F32)

    return pl.pallas_call(
        kernel,
        name="star",
        out_shape=[jax.ShapeDtypeStruct(forward_end.shape, F32), jax.ShapeDtypeStruct(potential.shape, F32)],
        in_specs=[pl.BlockSpec(memory_space=pltpu.HBM)] * 5,
        out_specs=[pl.BlockSpec(memory_space=pltpu.VMEM)] * 2,
        scratch_shapes=[
            pltpu.SMEM((2,), jnp.int32), pltpu.SMEM((2,), jnp.int32), full, full, full,
            v(ROWS, 2, YC[0], LANES), v(ROWS, 2, YC[1], LANES),
            v(8, YC[0], LANES), v(8, YC[1], LANES),
            v(10, 2, YC[0], LANES), v(10, 2, YC[1], LANES),
            v(10, 2, 2, YC[0], LANES), v(10, 2, 2, YC[1], LANES),
            v(10, 2, 2, YC[0], LANES), v(10, 2, 2, YC[1], LANES),
            full,
            v(2, ROWS, 24, LANES), v(2, 10, 24, LANES), v(2, ROWS, 8, LANES), v(2, 10, 8, LANES),
            v(2, 10, 2, 2, 8, LANES),
            v(2, 10, 2, YD, LANES), v(2, 10, 2, YD, LANES), v(2, 10, 2, YD, LANES),
            v(2, 2, ROWS, 64, 2 * LANES), v(2, 8, 64, 2 * LANES),
            dma((5,)), dma((32,)), dma((32,)), dma((24,)), dma((24,)), dma((48,)), dma((48,)),
        ],
        compiler_params=pltpu.CompilerParams(collective_id=0, has_side_effects=True, vmem_limit_bytes=51 << 20),
        cost_estimate=pl.CostEstimate(flops=20_000_000, bytes_accessed=5 << 20, transcendentals=1 << 19),
    )(species_label, arm_length, forward_end, partner_end, potential)


def solution(mesh):
    return jax.shard_map(
        local,
        mesh=mesh,
        in_specs=(
            P("arm", "sx", "sy", None),
            P("arm", "sx", "sy", None),
            P(None, "sx", "sy", None),
            P("arm"),
            P("arm"),
        ),
        out_specs=(P("arm", "sx", "sy", None), P(None, "sx", "sy", None)),
        check_vma=False,
    )
```

```python
import jax
import jax.numpy as jnp
from jax import lax
from jax.experimental import pallas as pl
from jax.experimental.pallas import tpu as pltpu
from jax.sharding import PartitionSpec as P

MESH = pl.DeviceIdType.MESH
F32 = jnp.float32
ROWS, NYL, LANES = 4, 128, 128
YD, Y0 = 160, 16
BOUNDS = ((40, 88), (8, 120), (0, 128))
RESULT = ((48, 80), (16, 112), (0, 128))
NC = len(BOUNDS)
DIRECT_P = (True, False, True)


def segments(bounds, k):
    lo, hi = bounds[k]
    if k == 0:
        return ((0, lo, hi - lo),)
    lo_in, hi_in = bounds[k - 1]
    return ((0, hi_in, hi - hi_in), (hi - hi_in, lo, lo_in - lo))


SEG = [segments(BOUNDS, k) for k in range(NC)]
YC = [sum(n for _, _, n in s) for s in SEG]
HALF = [((48, 16), (64, 16))] + [tuple((s, n) for _, s, n in segments(RESULT, k)) for k in range(1, NC)]
TILES = [tuple(range(BOUNDS[0][0] // 8, BOUNDS[0][1] // 8))]
for _k in range(1, NC):
    _end = 1 if _k == NC - 1 else 0
    TILES.append(
        tuple(range(BOUNDS[_k - 1][1] // 8 - 1, BOUNDS[_k][1] // 8 + _end))
        + tuple(range(BOUNDS[_k][0] // 8 - _end, BOUNDS[_k - 1][0] // 8 + 1))
    )
SEMS = 7 * NC + 3 - sum(DIRECT_P)
PLACE = {}
for _k in range(NC):
    for _o, _s, _n in SEG[_k]:
        for _b in range(0, _n, 8):
            PLACE[(_s + _b) // 8] = (_k, _o + _b)


def lanes(h):
    return slice(h * LANES, (h + 1) * LANES)


def kernel(lab_h, len_h, fwd, par, pot, conj, dens, *scratch):
    scratch = list(scratch)

    def take(n):
        out = scratch[:n]
        del scratch[:n]
        return out

    lab, length, fv, pv, uv, ifac, es, ce, pes, pe, gp, v1, v2, v3 = take(14)
    p, prx, pxx, pf, g, q = (take(NC) for _ in range(6))
    da, rxa = (take(NC) for _ in range(2))
    lsem, ssem, rsem = take(3)

    arm, sx, sy = lax.axis_index("arm"), lax.axis_index("sx"), lax.axis_index("sy")
    x, y = arm // 4, arm % 4
    ox = 1 - x
    ys = [y, y + 1 - 2 * (y % 2), (y + 2) % 4, 3 - y]
    peers = [((x, ox)[d // 4], ys[d % 4]) for d in range(8)]
    up, down, other = (sx + 1) % 32, (sx + 31) % 32, 1 - sy

    def arm_dev(d):
        return {"arm": peers[d][0] * 4 + peers[d][1]}

    around = [{"sx": up}, {"sx": down}, {"sy": other}, {"sx": up, "sy": other}, {"sx": down, "sy": other}]

    quarters = [pl.ds(r, 1) for r in range(ROWS)]
    for r in quarters:
        pltpu.make_async_copy(fwd.at[:, r], fv.at[:, r], lsem.at[0]).start()
    for i, (src, dst) in enumerate(((pot, uv), (lab_h, lab), (len_h, length), (par, pv))):
        pltpu.make_async_copy(src, dst, lsem.at[i + 1]).start()

    def loaded(i, src, dst):
        pltpu.make_async_copy(src, dst, lsem.at[i]).wait()

    groups = {}

    def send(group, src, dst, dev):
        n = groups.setdefault(group, len(groups))
        pltpu.make_async_remote_copy(
            src_ref=src, dst_ref=dst, send_sem=ssem.at[n], recv_sem=rsem.at[n], device_id=dev, device_id_type=MESH
        ).start()

    sizes = []

    def arrived(group, like):
        pltpu.make_async_copy(like, like, rsem.at[groups[group]]).wait()
        sizes.append((group, like))

    barrier = pltpu.get_barrier_semaphore()
    for d in range(1, 8):
        pl.semaphore_signal(barrier, inc=1, device_id=arm_dev(d), device_id_type=MESH)
    for dev in around:
        pl.semaphore_signal(barrier, inc=1, device_id=dev, device_id_type=MESH)

    loaded(0, fwd, fv)

    @pl.loop(0, ROWS)
    def _(r):
        for k in range(NC):
            for o, s, n in SEG[k]:
                for h in range(2):
                    p[k][r, h, o:o + n] = fv[0, r, s:s + n, lanes(h)] * fv[1, r, s:s + n, lanes(h)]

    def work_out(k):
        @pl.loop(0, ROWS)
        def _(r):
            for o, s, n in SEG[k]:
                for h in range(2):
                    for b in range(0, n, 8):
                        ya, oa = s + b, o + b
                        u0, u1 = (uv[i, r, ya:ya + 8, lanes(h)] for i in range(2))
                        for a in range(2):
                            e = jnp.exp(-0.5 * jnp.where(l[a], u1, u0))
                            ge = e / fv[a, r, ya:ya + 8, lanes(h)]
                            qe = (0.16 * e) * e
                            g[k][r + 3, a, h, oa:oa + 8] = ge
                            q[k][r + 3, a, h, oa:oa + 8] = qe
                            ifac[a, r, ya:ya + 8, lanes(h)] = 1.0 / e
                            i, j = a * 6 + h * 3, 12 + a * 4 + h * 2
                            if ya == 0:
                                es[0, r, i:i + 3] = ge[0:3]
                                es[0, r, j:j + 2] = qe[0:2]
                            if ya == NYL - 8:
                                es[1, r, i:i + 3] = ge[5:8]
                                es[1, r, j:j + 2] = qe[6:8]

    pl.semaphore_wait(barrier, 12)

    g_rows = ((pl.ds(4, 3), pl.ds(0, 3)), (pl.ds(3, 3), pl.ds(7, 3)))
    q_rows = ((pl.ds(5, 2), pl.ds(1, 2)), (pl.ds(3, 2), pl.ds(7, 2)))

    def edges(group, src, dst, corners):
        for side in range(2):
            send(group, src.at[side], dst.at[side, pl.ds(3, 4)], around[2])
            if corners:
                send(group, src.at[side, pl.ds(1, 3)], dst.at[side, pl.ds(0, 3)], around[3])
                send(group, src.at[side, pl.ds(0, 3)], dst.at[side, pl.ds(7, 3)], around[4])

    def forward_corners():
        arrived("edge", es)
        for side in range(2):
            send("corner", ce.at[side, pl.ds(4, 3)], ce.at[side, pl.ds(0, 3)], around[0])
            send("corner", ce.at[side, pl.ds(3, 3)], ce.at[side, pl.ds(7, 3)], around[1])

    def scatter(k):
        if DIRECT_P[k]:
            for d in range(1, 8):
                px, py = peers[d]
                send(f"rs{k}", p[k].at[py, px], prx[k].at[d], arm_dev(d))
        else:
            for d in (1, 2, 3):
                send(f"rs{k}", p[k].at[ys[d]], prx[k].at[pl.ds(2 * d, 2)], arm_dev(d))

    def coefficients(k):
        for i in range(2):
            send(f"coef{k}", g[k].at[g_rows[i][0]], g[k].at[g_rows[i][1]], around[i])
            send(f"coef{k}", q[k].at[q_rows[i][0]], q[k].at[q_rows[i][1]], around[i])

    def cross(k):
        if DIRECT_P[k]:
            return
        arrived(f"rs{k}", prx[k].at[pl.ds(2, 6)])
        for h in range(2):
            for b in range(0, YC[k], 16):
                c = slice(b, b + 16)
                prx[k][h, c] = (p[k][y, h, c] * prx[k][2 + h, c]) * (prx[k][4 + h, c] * prx[k][6 + h, c])
        send(f"xp{k}", prx[k].at[pl.ds(0, 2)], pxx[k], arm_dev(4))

    def gather(k):
        if DIRECT_P[k]:
            arrived(f"rs{k}", prx[k].at[pl.ds(1, 7)])
            for b in range(0, YC[k], 16):
                acc = p[k][y, x, b:b + 16]
                for d in range(1, 8):
                    acc = acc * prx[k][d, b:b + 16]
                pf[k][3 + y, x, b:b + 16] = acc
            mine = pf[k].at[3 + y, x]
            for d in range(1, 8):
                send(f"ag{k}", mine, mine, arm_dev(d))
        else:
            arrived(f"xp{k}", pxx[k])
            for h in range(2):
                for b in range(0, YC[k], 16):
                    pf[k][3 + y, h, b:b + 16] = prx[k][h, b:b + 16] * pxx[k][h, b:b + 16]
            mine = pf[k].at[3 + y]
            for d in (1, 2, 3):
                send(f"ag{k}", mine, mine, arm_dev(d))

    def product_halo(k):
        arrived(f"ag{k}", prx[k].at[pl.ds(1, 7) if DIRECT_P[k] else pl.ds(2, 6)])
        for i in range(2):
            send(f"ph{k}", pf[k].at[g_rows[i][0]], pf[k].at[g_rows[i][1]], around[i])
        if k == NC - 1:
            k0, o0 = PLACE[0]
            k1, o1 = PLACE[NYL // 8 - 1]
            for r in range(ROWS):
                for h in range(2):
                    pes[0, r, 3 * h:3 * h + 3] = pf[k0][r + 3, h, o0:o0 + 3]
                    pes[1, r, 3 * h:3 * h + 3] = pf[k1][r + 3, h, o1 + 5:o1 + 8]
            edges("pe", pes, pe, True)

    scatter(0)
    scatter(2)
    loaded(1, pot, uv)
    loaded(2, lab_h, lab)
    loaded(3, len_h, length)
    l = [lab[a] == 1 for a in range(2)]
    work_out(0)
    coefficients(0)
    work_out(2)
    scatter(1)
    coefficients(2)
    edges("edge", es, ce, False)
    work_out(1)
    gather(0)
    gather(2)
    coefficients(1)
    cross(1)
    forward_corners()
    gather(1)
    product_halo(0)
    product_halo(2)
    product_halo(1)

    lane = lax.broadcasted_iota(jnp.int32, (8, LANES), 1)
    first, last = lane == 0, lane == LANES - 1

    def q_tile(a, r, h, t):
        if t in (-1, 16):
            return gp[0 if t == 16 else 1, r, a, h]
        k, o = PLACE[t]
        return q[k][r, a, h, o:o + 8]

    def advance(src, a, r, t, active):
        b = Y0 + 8 * t
        v = [src[a, r, h, b:b + 8] for h in range(2)]
        right = [pltpu.roll(w, 1, 1) for w in v]
        left = [pltpu.roll(w, LANES - 1, 1) for w in v]
        out = []
        for h in range(2):
            s = src[a, r - 1, h, b:b + 8] + src[a, r + 1, h, b:b + 8]
            s = s + (src[a, r, h, b - 1:b + 7] + src[a, r, h, b + 1:b + 9])
            s = s + (jnp.where(first, right[1 - h], right[h]) + jnp.where(last, left[1 - h], left[h]))
            new = q_tile(a, r, h, t) * (0.25 * v[h] + s)
            out.append(jnp.where(active, new, v[h]))
        return out

    def steps(k):
        arrived(f"coef{k}", g[k])
        arrived(f"ph{k}", pf[k].at[pl.ds(0, 6)])
        if k == NC - 1:
            arrived("corner", ce.at[:, pl.ds(0, 6)])
            arrived("pe", pe)

        @pl.loop(0, 10)
        def _(r):
            for o, s, n in SEG[k]:
                for h in range(2):
                    f = pf[k][r, h, o:o + n]
                    for a in range(2):
                        v1[a, r, h, Y0 + s:Y0 + s + n] = f * g[k][r, a, h, o:o + n]
            if k == NC - 1:
                for side, b in ((0, Y0 + NYL), (1, Y0 - 3)):
                    for h in range(2):
                        f = pe[side, r, 3 * h:3 * h + 3]
                        for a in range(2):
                            i, j = a * 6 + h * 3, 12 + a * 4 + h * 2
                            v1[a, r, h, b:b + 3] = f * ce[side, r, i:i + 3]
                            gp[side, r, a, h, 6 * side:6 * side + 2] = ce[side, r, j:j + 2]

        for t, (src, dst) in enumerate(((v1, v2), (v2, v3))):
            act = [length[a] > t for a in range(2)]

            @pl.loop(1 + t, 9 - t)
            def _(r):
                for tile in TILES[k]:
                    b = Y0 + 8 * tile
                    for a in range(2):
                        out = advance(src, a, r, tile, act[a])
                        for h in range(2):
                            dst[a, r, h, b:b + 8] = out[h]

        act = [length[a] > 2 for a in range(2)]
        for i in (1, 2, 3, 0):
            r = ys[i]
            for half in range(2):
                s0, n0 = HALF[k][half]
                for m in range(0, n0, 8):
                    b = s0 + m
                    w = []
                    for a in range(2):
                        out = advance(v3, a, r + 3, b // 8, act[a])
                        ws = []
                        for h in range(2):
                            c = out[h] * ifac[a, r, b:b + 8, lanes(h)]
                            conj[a, r, b:b + 8, lanes(h)] = c
                            ws.append(c * pv[a, r, b:b + 8, lanes(h)])
                        w.append(ws)
                    for h in range(2):
                        zero = jnp.where(l[0], 0.0, w[0][h]) + jnp.where(l[1], 0.0, w[1][h])
                        one = jnp.where(l[0], w[0][h], 0.0) + jnp.where(l[1], w[1][h], 0.0)
                        o = m + half * n0
                        da[k][0, r, o:o + 8, lanes(h)] = zero
                        da[k][1, r, o:o + 8, lanes(h)] = one
            for j in (i, i + 4):
                if j:
                    px, py = peers[j]
                    send(f"drs{k}", da[k].at[px, py], rxa[k].at[j], arm_dev(j))

    def gather_density(k):
        arrived(f"drs{k}", rxa[k].at[pl.ds(1, 7)])
        o = 0
        for half, (s, n) in enumerate(HALF[k]):
            for h in range(2):
                for b in range(0, n, 8):
                    c = slice(o + b, o + b + 8)
                    acc = da[k][x, y, c, lanes(h)]
                    for d in range(1, 8):
                        acc = acc + rxa[k][d, c, lanes(h)]
                    dens[x, y, s + b:s + b + 8, lanes(h)] = acc
            o += n
            if k == 0 and half == 0:
                continue
            piece = dens.at[x, y, pl.ds(HALF[0][0][0], 2 * n) if k == 0 else pl.ds(s, n)]
            for d in range(1, 8):
                send(f"dag{k}", piece, piece, arm_dev(d))

    loaded(4, par, pv)
    for k in range(NC):
        steps(k)
    for k in range(NC):
        gather_density(k)
    for k in range(NC):
        arrived(f"dag{k}", rxa[k].at[pl.ds(1, 7)])
    for group, like in sizes:
        pltpu.make_async_copy(like, like, ssem.at[groups[group]]).wait()


def local(forward_end, partner_end, potential, species_label, arm_length):
    full = pltpu.VMEM((2, ROWS, NYL, 2 * LANES), F32)
    dma = pltpu.SemaphoreType.DMA

    def v(*shape):
        return pltpu.VMEM(shape, F32)

    wide = 2 * LANES
    nh = [h[0][1] for h in HALF]
    return pl.pallas_call(
        kernel,
        name="star",
        out_shape=[jax.ShapeDtypeStruct(forward_end.shape, F32), jax.ShapeDtypeStruct(potential.shape, F32)],
        in_specs=[pl.BlockSpec(memory_space=pl.ANY)] * 5,
        out_specs=[pl.BlockSpec(memory_space=pltpu.VMEM)] * 2,
        scratch_shapes=[
            pltpu.SMEM((2,), jnp.int32), pltpu.SMEM((2,), jnp.int32), full, full, full, full,
            v(2, ROWS, 24, LANES), v(2, 10, 24, LANES), v(2, ROWS, 8, LANES), v(2, 10, 8, LANES),
            v(2, 10, 2, 2, 8, LANES),
            v(2, 10, 2, YD, LANES), v(2, 10, 2, YD, LANES), v(2, 10, 2, YD, LANES),
        ]
        + [v(ROWS, 2, n, LANES) for n in YC]
        + [v(8, n, LANES) for n in YC]
        + [v(2, n, LANES) for n in YC]
        + [v(10, 2, n, LANES) for n in YC]
        + [v(10, 2, 2, n, LANES) for n in YC]
        + [v(10, 2, 2, n, LANES) for n in YC]
        + [v(2, ROWS, 2 * n, wide) for n in nh]
        + [v(8, 2 * n, wide) for n in nh]
        + [dma((n,)) for n in (5, SEMS, SEMS)],
        compiler_params=pltpu.CompilerParams(collective_id=0, has_side_effects=True, vmem_limit_bytes=51 << 20),
        cost_estimate=pl.CostEstimate(flops=20_000_000, bytes_accessed=5 << 20, transcendentals=1 << 19),
    )(species_label, arm_length, forward_end, partner_end, potential)


def solution(mesh):
    return jax.shard_map(
        local,
        mesh=mesh,
        in_specs=(
            P("arm", "sx", "sy", None),
            P("arm", "sx", "sy", None),
            P(None, "sx", "sy", None),
            P("arm"),
            P("arm"),
        ),
        out_specs=(P("arm", "sx", "sy", None), P(None, "sx", "sy", None)),
        check_vma=False,
    )
```

```python
import jax
import jax.numpy as jnp
from jax import lax
from jax.experimental import pallas as pl
from jax.experimental.pallas import tpu as pltpu
from jax.sharding import PartitionSpec as P

MESH = pl.DeviceIdType.MESH
F32 = jnp.float32
ROWS, NYL, LANES = 4, 128, 128
YD, Y0 = 160, 16
BOUNDS = ((32, 96), (8, 120), (0, 128))
RESULT = ((40, 88), (16, 112), (0, 128))
NC = len(BOUNDS)
TWO_LEVEL = (True, True, False)
DIRECT_P = (True, False, True)


def segments(bounds, k):
    lo, hi = bounds[k]
    if k == 0:
        return ((0, lo, hi - lo),)
    lo_in, hi_in = bounds[k - 1]
    return ((0, hi_in, hi - hi_in), (hi - hi_in, lo, lo_in - lo))


SEG = [segments(BOUNDS, k) for k in range(NC)]
YC = [sum(n for _, _, n in s) for s in SEG]
_lo, _n = RESULT[0][0], (RESULT[0][1] - RESULT[0][0]) // 2
HALF = [((_lo, _n), (_lo + _n, _n))] + [tuple((s, n) for _, s, n in segments(RESULT, k)) for k in range(1, NC)]
TILES = [tuple(range(BOUNDS[0][0] // 8, BOUNDS[0][1] // 8))]
for _k in range(1, NC):
    _end = 1 if _k == NC - 1 else 0
    TILES.append(
        tuple(range(BOUNDS[_k - 1][1] // 8 - 1, BOUNDS[_k][1] // 8 + _end))
        + tuple(range(BOUNDS[_k][0] // 8 - _end, BOUNDS[_k - 1][0] // 8 + 1))
    )
SEMS = 7 * NC + 3 - sum(DIRECT_P) + sum(TWO_LEVEL)
PLACE = {}
for _k in range(NC):
    for _o, _s, _n in SEG[_k]:
        for _b in range(0, _n, 8):
            PLACE[(_s + _b) // 8] = (_k, _o + _b)


def lanes(h):
    return slice(h * LANES, (h + 1) * LANES)


def kernel(lab_h, len_h, fwd, par, pot, conj, dens, *scratch):
    scratch = list(scratch)

    def take(n):
        out = scratch[:n]
        del scratch[:n]
        return out

    lab, length, fv, pv, uv, ifac, es, ce, pes, pe, gp, v1, v2, v3 = take(14)
    p, prx, pxx, pf, g, q = (take(NC) for _ in range(6))
    da, rxa = (take(NC) for _ in range(2))
    lsem, ssem, rsem = take(3)

    arm, sx, sy = lax.axis_index("arm"), lax.axis_index("sx"), lax.axis_index("sy")
    x, y = arm // 4, arm % 4
    ox = 1 - x
    ys = [y, y + 1 - 2 * (y % 2), (y + 2) % 4, 3 - y]
    peers = [((x, ox)[d // 4], ys[d % 4]) for d in range(8)]
    up, down, other = (sx + 1) % 32, (sx + 31) % 32, 1 - sy

    def arm_dev(d):
        return {"arm": peers[d][0] * 4 + peers[d][1]}

    around = [{"sx": up}, {"sx": down}, {"sy": other}, {"sx": up, "sy": other}, {"sx": down, "sy": other}]

    quarters = [pl.ds(r, 1) for r in range(ROWS)]
    for r in quarters:
        pltpu.make_async_copy(fwd.at[:, r], fv.at[:, r], lsem.at[0]).start()
    for i, (src, dst) in enumerate(((pot, uv), (lab_h, lab), (len_h, length), (par, pv))):
        pltpu.make_async_copy(src, dst, lsem.at[i + 1]).start()

    def loaded(i, src, dst):
        pltpu.make_async_copy(src, dst, lsem.at[i]).wait()

    groups = {}

    def send(group, src, dst, dev):
        n = groups.setdefault(group, len(groups))
        pltpu.make_async_remote_copy(
            src_ref=src, dst_ref=dst, send_sem=ssem.at[n], recv_sem=rsem.at[n], device_id=dev, device_id_type=MESH
        ).start()

    sizes = []

    def arrived(group, like):
        pltpu.make_async_copy(like, like, rsem.at[groups[group]]).wait()
        sizes.append((group, like))

    barrier = pltpu.get_barrier_semaphore()
    for d in range(1, 8):
        pl.semaphore_signal(barrier, inc=1, device_id=arm_dev(d), device_id_type=MESH)
    for dev in around:
        pl.semaphore_signal(barrier, inc=1, device_id=dev, device_id_type=MESH)

    loaded(0, fwd, fv)

    @pl.loop(0, ROWS)
    def _(r):
        for k in range(NC):
            for o, s, n in SEG[k]:
                for h in range(2):
                    p[k][r, h, o:o + n] = fv[0, r, s:s + n, lanes(h)] * fv[1, r, s:s + n, lanes(h)]

    def work_out(k):
        @pl.loop(0, ROWS)
        def _(r):
            for o, s, n in SEG[k]:
                for h in range(2):
                    for b in range(0, n, 8):
                        ya, oa = s + b, o + b
                        u0, u1 = (uv[i, r, ya:ya + 8, lanes(h)] for i in range(2))
                        for a in range(2):
                            e = jnp.exp(-0.5 * jnp.where(l[a], u1, u0))
                            ge = e / fv[a, r, ya:ya + 8, lanes(h)]
                            qe = (0.16 * e) * e
                            g[k][r + 3, a, h, oa:oa + 8] = ge
                            q[k][r + 3, a, h, oa:oa + 8] = qe
                            ifac[a, r, ya:ya + 8, lanes(h)] = 1.0 / e
                            i, j = a * 6 + h * 3, 12 + a * 4 + h * 2
                            if ya == 0:
                                es[0, r, i:i + 3] = ge[0:3]
                                es[0, r, j:j + 2] = qe[0:2]
                            if ya == NYL - 8:
                                es[1, r, i:i + 3] = ge[5:8]
                                es[1, r, j:j + 2] = qe[6:8]

    pl.semaphore_wait(barrier, 12)

    g_rows = ((pl.ds(4, 3), pl.ds(0, 3)), (pl.ds(3, 3), pl.ds(7, 3)))
    q_rows = ((pl.ds(5, 2), pl.ds(1, 2)), (pl.ds(3, 2), pl.ds(7, 2)))

    def edges(group, src, dst, corners):
        for side in range(2):
            send(group, src.at[side], dst.at[side, pl.ds(3, 4)], around[2])
            if corners:
                send(group, src.at[side, pl.ds(1, 3)], dst.at[side, pl.ds(0, 3)], around[3])
                send(group, src.at[side, pl.ds(0, 3)], dst.at[side, pl.ds(7, 3)], around[4])

    def forward_corners():
        arrived("edge", es)
        for side in range(2):
            send("corner", ce.at[side, pl.ds(4, 3)], ce.at[side, pl.ds(0, 3)], around[0])
            send("corner", ce.at[side, pl.ds(3, 3)], ce.at[side, pl.ds(7, 3)], around[1])

    def scatter(k):
        if DIRECT_P[k]:
            for d in range(1, 8):
                px, py = peers[d]
                send(f"rs{k}", p[k].at[py, px], prx[k].at[d], arm_dev(d))
        else:
            for d in (1, 2, 3):
                send(f"rs{k}", p[k].at[ys[d]], prx[k].at[pl.ds(2 * d, 2)], arm_dev(d))

    def coefficients(k):
        for i in range(2):
            send(f"coef{k}", g[k].at[g_rows[i][0]], g[k].at[g_rows[i][1]], around[i])
            send(f"coef{k}", q[k].at[q_rows[i][0]], q[k].at[q_rows[i][1]], around[i])

    def cross(k):
        if DIRECT_P[k]:
            return
        arrived(f"rs{k}", prx[k].at[pl.ds(2, 6)])
        for h in range(2):
            for b in range(0, YC[k], 16):
                c = slice(b, b + 16)
                prx[k][h, c] = (p[k][y, h, c] * prx[k][2 + h, c]) * (prx[k][4 + h, c] * prx[k][6 + h, c])
        send(f"xp{k}", prx[k].at[pl.ds(0, 2)], pxx[k], arm_dev(4))

    def gather(k):
        if DIRECT_P[k]:
            arrived(f"rs{k}", prx[k].at[pl.ds(1, 7)])
            for b in range(0, YC[k], 16):
                acc = p[k][y, x, b:b + 16]
                for d in range(1, 8):
                    acc = acc * prx[k][d, b:b + 16]
                pf[k][3 + y, x, b:b + 16] = acc
            mine = pf[k].at[3 + y, x]
            for d in range(1, 8):
                send(f"ag{k}", mine, mine, arm_dev(d))
        else:
            arrived(f"xp{k}", pxx[k])
            for h in range(2):
                for b in range(0, YC[k], 16):
                    pf[k][3 + y, h, b:b + 16] = prx[k][h, b:b + 16] * pxx[k][h, b:b + 16]
            mine = pf[k].at[3 + y]
            for d in (1, 2, 3):
                send(f"ag{k}", mine, mine, arm_dev(d))

    def product_halo(k):
        arrived(f"ag{k}", prx[k].at[pl.ds(1, 7) if DIRECT_P[k] else pl.ds(2, 6)])
        for i in range(2):
            send(f"ph{k}", pf[k].at[g_rows[i][0]], pf[k].at[g_rows[i][1]], around[i])
        if k == NC - 1:
            k0, o0 = PLACE[0]
            k1, o1 = PLACE[NYL // 8 - 1]
            for r in range(ROWS):
                for h in range(2):
                    pes[0, r, 3 * h:3 * h + 3] = pf[k0][r + 3, h, o0:o0 + 3]
                    pes[1, r, 3 * h:3 * h + 3] = pf[k1][r + 3, h, o1 + 5:o1 + 8]
            edges("pe", pes, pe, True)

    scatter(0)
    scatter(2)
    loaded(1, pot, uv)
    loaded(2, lab_h, lab)
    loaded(3, len_h, length)
    l = [lab[a] == 1 for a in range(2)]
    work_out(0)
    coefficients(0)
    work_out(2)
    scatter(1)
    coefficients(2)
    edges("edge", es, ce, False)
    work_out(1)
    gather(0)
    gather(2)
    coefficients(1)
    cross(1)
    forward_corners()
    gather(1)
    product_halo(0)
    product_halo(2)
    product_halo(1)

    lane = lax.broadcasted_iota(jnp.int32, (8, LANES), 1)
    first, last = lane == 0, lane == LANES - 1

    def q_tile(a, r, h, t):
        if t in (-1, 16):
            return gp[0 if t == 16 else 1, r, a, h]
        k, o = PLACE[t]
        return q[k][r, a, h, o:o + 8]

    def advance(src, a, r, t, active):
        b = Y0 + 8 * t
        v = [src[a, r, h, b:b + 8] for h in range(2)]
        right = [pltpu.roll(w, 1, 1) for w in v]
        left = [pltpu.roll(w, LANES - 1, 1) for w in v]
        out = []
        for h in range(2):
            s = src[a, r - 1, h, b:b + 8] + src[a, r + 1, h, b:b + 8]
            s = s + (src[a, r, h, b - 1:b + 7] + src[a, r, h, b + 1:b + 9])
            s = s + (jnp.where(first, right[1 - h], right[h]) + jnp.where(last, left[1 - h], left[h]))
            new = q_tile(a, r, h, t) * (0.25 * v[h] + s)
            out.append(jnp.where(active, new, v[h]))
        return out

    def steps(k):
        arrived(f"coef{k}", g[k])
        arrived(f"ph{k}", pf[k].at[pl.ds(0, 6)])
        if k == NC - 1:
            arrived("corner", ce.at[:, pl.ds(0, 6)])
            arrived("pe", pe)

        @pl.loop(0, 10)
        def _(r):
            for o, s, n in SEG[k]:
                for h in range(2):
                    f = pf[k][r, h, o:o + n]
                    for a in range(2):
                        v1[a, r, h, Y0 + s:Y0 + s + n] = f * g[k][r, a, h, o:o + n]
            if k == NC - 1:
                for side, b in ((0, Y0 + NYL), (1, Y0 - 3)):
                    for h in range(2):
                        f = pe[side, r, 3 * h:3 * h + 3]
                        for a in range(2):
                            i, j = a * 6 + h * 3, 12 + a * 4 + h * 2
                            v1[a, r, h, b:b + 3] = f * ce[side, r, i:i + 3]
                            gp[side, r, a, h, 6 * side:6 * side + 2] = ce[side, r, j:j + 2]

        for t, (src, dst) in enumerate(((v1, v2), (v2, v3))):
            act = [length[a] > t for a in range(2)]

            @pl.loop(1 + t, 9 - t)
            def _(r):
                for tile in TILES[k]:
                    b = Y0 + 8 * tile
                    for a in range(2):
                        out = advance(src, a, r, tile, act[a])
                        for h in range(2):
                            dst[a, r, h, b:b + 8] = out[h]

        act = [length[a] > 2 for a in range(2)]
        for i in (1, 2, 3, 0):
            r = ys[i]
            for half in range(2):
                s0, n0 = HALF[k][half]
                for m in range(0, n0, 8):
                    b = s0 + m
                    w = []
                    for a in range(2):
                        out = advance(v3, a, r + 3, b // 8, act[a])
                        ws = []
                        for h in range(2):
                            c = out[h] * ifac[a, r, b:b + 8, lanes(h)]
                            conj[a, r, b:b + 8, lanes(h)] = c
                            ws.append(c * pv[a, r, b:b + 8, lanes(h)])
                        w.append(ws)
                    for h in range(2):
                        zero = jnp.where(l[0], 0.0, w[0][h]) + jnp.where(l[1], 0.0, w[1][h])
                        one = jnp.where(l[0], w[0][h], 0.0) + jnp.where(l[1], w[1][h], 0.0)
                        o = m + half * n0
                        da[k][0, r, o:o + 8, lanes(h)] = zero
                        da[k][1, r, o:o + 8, lanes(h)] = one
            for j in (i, i + 4):
                if j:
                    px, py = peers[j]
                    send(f"drs{k}", da[k].at[px, py], rxa[k].at[j], arm_dev(j))

    def gather_density(k):
        arrived(f"drs{k}", rxa[k].at[pl.ds(1, 7)])
        o = 0
        for s, n in HALF[k]:
            for h in range(2):
                for b in range(0, n, 8):
                    c = slice(o + b, o + b + 8)
                    acc = da[k][x, y, c, lanes(h)]
                    for d in range(1, 8):
                        acc = acc + rxa[k][d, c, lanes(h)]
                    dens[x, y, s + b:s + b + 8, lanes(h)] = acc
            o += n
        parts = [dens.at[x, y, pl.ds(s, n)] for s, n in HALF[k]]
        if TWO_LEVEL[k]:
            send(f"first{k}", parts[1], parts[1], arm_dev(4))
            for d in (1, 2, 3):
                send(f"first{k}", parts[0], parts[0], arm_dev(d))
            send(f"dag{k}", parts[0], parts[0], arm_dev(4))
            for d in (1, 2, 3):
                send(f"dag{k}", parts[1], parts[1], arm_dev(d))
        else:
            for piece in parts:
                for d in range(1, 8):
                    send(f"dag{k}", piece, piece, arm_dev(d))

    def pass_on(k):
        if TWO_LEVEL[k]:
            (s0, n0), (s1, n1) = HALF[k]
            arrived(f"first{k}", rxa[k].at[pl.ds(1, 2)])
            for d in (1, 2, 3):
                piece = dens.at[x, ys[d], pl.ds(s0, n0)]
                send(f"dag{k}", piece, piece, arm_dev(4))
            piece = dens.at[ox, y, pl.ds(s1, n1)]
            for d in (1, 2, 3):
                send(f"dag{k}", piece, piece, arm_dev(d))

    loaded(4, par, pv)
    for k in range(NC):
        steps(k)
    for k in range(NC):
        gather_density(k)
    for k in range(NC):
        pass_on(k)
    for k in range(NC):
        arrived(f"dag{k}", rxa[k].at[pl.ds(1, 5 if TWO_LEVEL[k] else 7)])
    for group, like in sizes:
        pltpu.make_async_copy(like, like, ssem.at[groups[group]]).wait()


def local(forward_end, partner_end, potential, species_label, arm_length):
    full = pltpu.VMEM((2, ROWS, NYL, 2 * LANES), F32)
    dma = pltpu.SemaphoreType.DMA

    def v(*shape):
        return pltpu.VMEM(shape, F32)

    wide = 2 * LANES
    nh = [h[0][1] for h in HALF]
    return pl.pallas_call(
        kernel,
        name="star",
        out_shape=[jax.ShapeDtypeStruct(forward_end.shape, F32), jax.ShapeDtypeStruct(potential.shape, F32)],
        in_specs=[pl.BlockSpec(memory_space=pl.ANY)] * 5,
        out_specs=[pl.BlockSpec(memory_space=pltpu.VMEM)] * 2,
        scratch_shapes=[
            pltpu.SMEM((2,), jnp.int32), pltpu.SMEM((2,), jnp.int32), full, full, full, full,
            v(2, ROWS, 24, LANES), v(2, 10, 24, LANES), v(2, ROWS, 8, LANES), v(2, 10, 8, LANES),
            v(2, 10, 2, 2, 8, LANES),
            v(2, 10, 2, YD, LANES), v(2, 10, 2, YD, LANES), v(2, 10, 2, YD, LANES),
        ]
        + [v(ROWS, 2, n, LANES) for n in YC]
        + [v(8, n, LANES) for n in YC]
        + [v(2, n, LANES) for n in YC]
        + [v(10, 2, n, LANES) for n in YC]
        + [v(10, 2, 2, n, LANES) for n in YC]
        + [v(10, 2, 2, n, LANES) for n in YC]
        + [v(2, ROWS, 2 * n, wide) for n in nh]
        + [v(8, 2 * n, wide) for n in nh]
        + [dma((n,)) for n in (5, SEMS, SEMS)],
        compiler_params=pltpu.CompilerParams(collective_id=0, has_side_effects=True, vmem_limit_bytes=51 << 20),
        cost_estimate=pl.CostEstimate(flops=20_000_000, bytes_accessed=5 << 20, transcendentals=1 << 19),
    )(species_label, arm_length, forward_end, partner_end, potential)


def solution(mesh):
    return jax.shard_map(
        local,
        mesh=mesh,
        in_specs=(
            P("arm", "sx", "sy", None),
            P("arm", "sx", "sy", None),
            P(None, "sx", "sy", None),
            P("arm"),
            P("arm"),
        ),
        out_specs=(P("arm", "sx", "sy", None), P(None, "sx", "sy", None)),
        check_vma=False,
    )
```

```python
import jax
import jax.numpy as jnp
from jax import lax
from jax.experimental import pallas as pl
from jax.experimental.pallas import tpu as pltpu
from jax.sharding import PartitionSpec as P

MESH = pl.DeviceIdType.MESH
F32 = jnp.float32
ROWS, NYL, LANES = 4, 128, 128
YD, Y0 = 160, 16
BOUNDS = ((32, 96), (8, 120), (0, 128))
RESULT = ((40, 88), (16, 112), (0, 128))
NC = len(BOUNDS)
TWO_LEVEL = (True, True, False)
DIRECT_P = (True, False, True)


def segments(bounds, k):
    lo, hi = bounds[k]
    if k == 0:
        return ((0, lo, hi - lo),)
    lo_in, hi_in = bounds[k - 1]
    return ((0, hi_in, hi - hi_in), (hi - hi_in, lo, lo_in - lo))


SEG = [segments(BOUNDS, k) for k in range(NC)]
YC = [sum(n for _, _, n in s) for s in SEG]
_lo, _n = RESULT[0][0], (RESULT[0][1] - RESULT[0][0]) // 2
HALF = [((_lo, _n), (_lo + _n, _n))] + [tuple((s, n) for _, s, n in segments(RESULT, k)) for k in range(1, NC)]
TILES = [tuple(range(BOUNDS[0][0] // 8, BOUNDS[0][1] // 8))]
for _k in range(1, NC):
    _end = 1 if _k == NC - 1 else 0
    TILES.append(
        tuple(range(BOUNDS[_k - 1][1] // 8 - 1, BOUNDS[_k][1] // 8 + _end))
        + tuple(range(BOUNDS[_k][0] // 8 - _end, BOUNDS[_k - 1][0] // 8 + 1))
    )
SEMS = 7 * NC + 3 - sum(DIRECT_P) + sum(TWO_LEVEL)
PLACE = {}
for _k in range(NC):
    for _o, _s, _n in SEG[_k]:
        for _b in range(0, _n, 8):
            PLACE[(_s + _b) // 8] = (_k, _o + _b)


def lanes(h):
    return slice(h * LANES, (h + 1) * LANES)


def kernel(label_length, fwd, par, pot, conj, dens, *scratch):
    scratch = list(scratch)

    def take(n):
        out = scratch[:n]
        del scratch[:n]
        return out

    scalars, fv, pv, uv, ifac, es, ce, pes, pe, gp, v1, v2, v3 = take(13)
    p, prx, pxx, pf, g, q = (take(NC) for _ in range(6))
    da, rxa = (take(NC) for _ in range(2))
    lsem, ssem, rsem = take(3)

    arm, sx, sy = lax.axis_index("arm"), lax.axis_index("sx"), lax.axis_index("sy")
    x, y = arm // 4, arm % 4
    ox = 1 - x
    ys = [y, y + 1 - 2 * (y % 2), (y + 2) % 4, 3 - y]
    peers = [((x, ox)[d // 4], ys[d % 4]) for d in range(8)]
    up, down, other = (sx + 1) % 32, (sx + 31) % 32, 1 - sy

    def arm_dev(d):
        return {"arm": peers[d][0] * 4 + peers[d][1]}

    around = [{"sx": up}, {"sx": down}, {"sy": other}, {"sx": up, "sy": other}, {"sx": down, "sy": other}]

    quarters = [pl.ds(r, 1) for r in range(ROWS)]
    for r in quarters:
        pltpu.make_async_copy(fwd.at[:, r], fv.at[:, r], lsem.at[0]).start()
    for i, (src, dst) in enumerate(((pot, uv), (label_length, scalars), (par, pv))):
        pltpu.make_async_copy(src, dst, lsem.at[i + 1]).start()

    def loaded(i, src, dst):
        pltpu.make_async_copy(src, dst, lsem.at[i]).wait()

    groups = {}

    def send(group, src, dst, dev):
        n = groups.setdefault(group, len(groups))
        pltpu.make_async_remote_copy(
            src_ref=src, dst_ref=dst, send_sem=ssem.at[n], recv_sem=rsem.at[n], device_id=dev, device_id_type=MESH
        ).start()

    sizes = []

    def arrived(group, like):
        pltpu.make_async_copy(like, like, rsem.at[groups[group]]).wait()
        sizes.append((group, like))

    barrier = pltpu.get_barrier_semaphore()
    for d in range(1, 8):
        pl.semaphore_signal(barrier, inc=1, device_id=arm_dev(d), device_id_type=MESH)
    for dev in around:
        pl.semaphore_signal(barrier, inc=1, device_id=dev, device_id_type=MESH)

    loaded(0, fwd, fv)

    @pl.loop(0, ROWS)
    def _(r):
        for k in range(NC):
            for o, s, n in SEG[k]:
                for h in range(2):
                    p[k][r, h, o:o + n] = fv[0, r, s:s + n, lanes(h)] * fv[1, r, s:s + n, lanes(h)]

    def work_out(k):
        @pl.loop(0, ROWS)
        def _(r):
            for o, s, n in SEG[k]:
                for h in range(2):
                    for b in range(0, n, 8):
                        ya, oa = s + b, o + b
                        u0, u1 = (uv[i, r, ya:ya + 8, lanes(h)] for i in range(2))
                        for a in range(2):
                            e = jnp.exp(-0.5 * jnp.where(l[a], u1, u0))
                            ge = e / fv[a, r, ya:ya + 8, lanes(h)]
                            qe = (0.16 * e) * e
                            g[k][r + 3, a, h, oa:oa + 8] = ge
                            q[k][r + 3, a, h, oa:oa + 8] = qe
                            ifac[a, r, ya:ya + 8, lanes(h)] = 1.0 / e
                            i, j = a * 6 + h * 3, 12 + a * 4 + h * 2
                            if ya == 0:
                                es[0, r, i:i + 3] = ge[0:3]
                                es[0, r, j:j + 2] = qe[0:2]
                            if ya == NYL - 8:
                                es[1, r, i:i + 3] = ge[5:8]
                                es[1, r, j:j + 2] = qe[6:8]

    pl.semaphore_wait(barrier, 12)

    g_rows = ((pl.ds(4, 3), pl.ds(0, 3)), (pl.ds(3, 3), pl.ds(7, 3)))
    q_rows = ((pl.ds(5, 2), pl.ds(1, 2)), (pl.ds(3, 2), pl.ds(7, 2)))

    def edges(group, src, dst, corners):
        for side in range(2):
            send(group, src.at[side], dst.at[side, pl.ds(3, 4)], around[2])
            if corners:
                send(group, src.at[side, pl.ds(1, 3)], dst.at[side, pl.ds(0, 3)], around[3])
                send(group, src.at[side, pl.ds(0, 3)], dst.at[side, pl.ds(7, 3)], around[4])

    def forward_corners():
        arrived("edge", es)
        for side in range(2):
            send("corner", ce.at[side, pl.ds(4, 3)], ce.at[side, pl.ds(0, 3)], around[0])
            send("corner", ce.at[side, pl.ds(3, 3)], ce.at[side, pl.ds(7, 3)], around[1])

    def scatter(k):
        if DIRECT_P[k]:
            for d in range(1, 8):
                px, py = peers[d]
                send(f"rs{k}", p[k].at[py, px], prx[k].at[d], arm_dev(d))
        else:
            for d in (1, 2, 3):
                send(f"rs{k}", p[k].at[ys[d]], prx[k].at[pl.ds(2 * d, 2)], arm_dev(d))

    def coefficients(k):
        for i in range(2):
            send(f"coef{k}", g[k].at[g_rows[i][0]], g[k].at[g_rows[i][1]], around[i])
            send(f"coef{k}", q[k].at[q_rows[i][0]], q[k].at[q_rows[i][1]], around[i])

    def cross(k):
        if DIRECT_P[k]:
            return
        arrived(f"rs{k}", prx[k].at[pl.ds(2, 6)])
        for h in range(2):
            for b in range(0, YC[k], 16):
                c = slice(b, b + 16)
                prx[k][h, c] = (p[k][y, h, c] * prx[k][2 + h, c]) * (prx[k][4 + h, c] * prx[k][6 + h, c])
        send(f"xp{k}", prx[k].at[pl.ds(0, 2)], pxx[k], arm_dev(4))

    def gather(k):
        if DIRECT_P[k]:
            arrived(f"rs{k}", prx[k].at[pl.ds(1, 7)])
            for b in range(0, YC[k], 16):
                acc = p[k][y, x, b:b + 16]
                for d in range(1, 8):
                    acc = acc * prx[k][d, b:b + 16]
                pf[k][3 + y, x, b:b + 16] = acc
            mine = pf[k].at[3 + y, x]
            for d in range(1, 8):
                send(f"ag{k}", mine, mine, arm_dev(d))
        else:
            arrived(f"xp{k}", pxx[k])
            for h in range(2):
                for b in range(0, YC[k], 16):
                    pf[k][3 + y, h, b:b + 16] = prx[k][h, b:b + 16] * pxx[k][h, b:b + 16]
            mine = pf[k].at[3 + y]
            for d in (1, 2, 3):
                send(f"ag{k}", mine, mine, arm_dev(d))

    def product_halo(k):
        arrived(f"ag{k}", prx[k].at[pl.ds(1, 7) if DIRECT_P[k] else pl.ds(2, 6)])
        for i in range(2):
            send(f"ph{k}", pf[k].at[g_rows[i][0]], pf[k].at[g_rows[i][1]], around[i])
        if k == NC - 1:
            k0, o0 = PLACE[0]
            k1, o1 = PLACE[NYL // 8 - 1]
            for r in range(ROWS):
                for h in range(2):
                    pes[0, r, 3 * h:3 * h + 3] = pf[k0][r + 3, h, o0:o0 + 3]
                    pes[1, r, 3 * h:3 * h + 3] = pf[k1][r + 3, h, o1 + 5:o1 + 8]
            edges("pe", pes, pe, True)

    scatter(0)
    scatter(2)
    loaded(1, pot, uv)
    loaded(2, label_length, scalars)
    l = [scalars[a] == 1 for a in range(2)]
    work_out(0)
    coefficients(0)
    work_out(2)
    scatter(1)
    coefficients(2)
    edges("edge", es, ce, False)
    work_out(1)
    gather(0)
    gather(2)
    coefficients(1)
    cross(1)
    forward_corners()
    gather(1)
    product_halo(0)
    product_halo(2)
    product_halo(1)

    lane = lax.broadcasted_iota(jnp.int32, (8, LANES), 1)
    first, last = lane == 0, lane == LANES - 1

    def q_tile(a, r, h, t):
        if t in (-1, 16):
            return gp[0 if t == 16 else 1, r, a, h]
        k, o = PLACE[t]
        return q[k][r, a, h, o:o + 8]

    def advance(src, a, r, t, active):
        b = Y0 + 8 * t
        v = [src[a, r, h, b:b + 8] for h in range(2)]
        right = [pltpu.roll(w, 1, 1) for w in v]
        left = [pltpu.roll(w, LANES - 1, 1) for w in v]
        out = []
        for h in range(2):
            s = src[a, r - 1, h, b:b + 8] + src[a, r + 1, h, b:b + 8]
            s = s + (src[a, r, h, b - 1:b + 7] + src[a, r, h, b + 1:b + 9])
            s = s + (jnp.where(first, right[1 - h], right[h]) + jnp.where(last, left[1 - h], left[h]))
            new = q_tile(a, r, h, t) * (0.25 * v[h] + s)
            out.append(jnp.where(active, new, v[h]))
        return out

    def steps(k):
        arrived(f"coef{k}", g[k])
        arrived(f"ph{k}", pf[k].at[pl.ds(0, 6)])
        if k == NC - 1:
            arrived("corner", ce.at[:, pl.ds(0, 6)])
            arrived("pe", pe)

        @pl.loop(0, 10)
        def _(r):
            for o, s, n in SEG[k]:
                for h in range(2):
                    f = pf[k][r, h, o:o + n]
                    for a in range(2):
                        v1[a, r, h, Y0 + s:Y0 + s + n] = f * g[k][r, a, h, o:o + n]
            if k == NC - 1:
                for side, b in ((0, Y0 + NYL), (1, Y0 - 3)):
                    for h in range(2):
                        f = pe[side, r, 3 * h:3 * h + 3]
                        for a in range(2):
                            i, j = a * 6 + h * 3, 12 + a * 4 + h * 2
                            v1[a, r, h, b:b + 3] = f * ce[side, r, i:i + 3]
                            gp[side, r, a, h, 6 * side:6 * side + 2] = ce[side, r, j:j + 2]

        for t, (src, dst) in enumerate(((v1, v2), (v2, v3))):
            act = [scalars[2 + a] > t for a in range(2)]

            @pl.loop(1 + t, 9 - t)
            def _(r):
                for tile in TILES[k]:
                    b = Y0 + 8 * tile
                    for a in range(2):
                        out = advance(src, a, r, tile, act[a])
                        for h in range(2):
                            dst[a, r, h, b:b + 8] = out[h]

        act = [scalars[2 + a] > 2 for a in range(2)]
        for i in (1, 2, 3, 0):
            r = ys[i]
            for half in range(2):
                s0, n0 = HALF[k][half]
                for m in range(0, n0, 8):
                    b = s0 + m
                    w = []
                    for a in range(2):
                        out = advance(v3, a, r + 3, b // 8, act[a])
                        ws = []
                        for h in range(2):
                            c = out[h] * ifac[a, r, b:b + 8, lanes(h)]
                            conj[a, r, b:b + 8, lanes(h)] = c
                            ws.append(c * pv[a, r, b:b + 8, lanes(h)])
                        w.append(ws)
                    for h in range(2):
                        zero = jnp.where(l[0], 0.0, w[0][h]) + jnp.where(l[1], 0.0, w[1][h])
                        one = jnp.where(l[0], w[0][h], 0.0) + jnp.where(l[1], w[1][h], 0.0)
                        o = m + half * n0
                        da[k][0, r, o:o + 8, lanes(h)] = zero
                        da[k][1, r, o:o + 8, lanes(h)] = one
            for j in (i, i + 4):
                if j:
                    px, py = peers[j]
                    send(f"drs{k}", da[k].at[px, py], rxa[k].at[j], arm_dev(j))

    def gather_density(k):
        arrived(f"drs{k}", rxa[k].at[pl.ds(1, 7)])
        o = 0
        for s, n in HALF[k]:
            for h in range(2):
                for b in range(0, n, 8):
                    c = slice(o + b, o + b + 8)
                    acc = da[k][x, y, c, lanes(h)]
                    for d in range(1, 8):
                        acc = acc + rxa[k][d, c, lanes(h)]
                    dens[x, y, s + b:s + b + 8, lanes(h)] = acc
            o += n
        parts = [dens.at[x, y, pl.ds(s, n)] for s, n in HALF[k]]
        if TWO_LEVEL[k]:
            send(f"first{k}", parts[1], parts[1], arm_dev(4))
            for d in (1, 2, 3):
                send(f"first{k}", parts[0], parts[0], arm_dev(d))
            send(f"dag{k}", parts[0], parts[0], arm_dev(4))
            for d in (1, 2, 3):
                send(f"dag{k}", parts[1], parts[1], arm_dev(d))
        else:
            for piece in parts:
                for d in range(1, 8):
                    send(f"dag{k}", piece, piece, arm_dev(d))

    def pass_on(k):
        if TWO_LEVEL[k]:
            (s0, n0), (s1, n1) = HALF[k]
            arrived(f"first{k}", rxa[k].at[pl.ds(1, 2)])
            for d in (1, 2, 3):
                piece = dens.at[x, ys[d], pl.ds(s0, n0)]
                send(f"dag{k}", piece, piece, arm_dev(4))
            piece = dens.at[ox, y, pl.ds(s1, n1)]
            for d in (1, 2, 3):
                send(f"dag{k}", piece, piece, arm_dev(d))

    loaded(3, par, pv)
    for k in range(NC):
        steps(k)
    for k in range(NC):
        gather_density(k)
    for k in range(NC):
        pass_on(k)
    for k in range(NC):
        arrived(f"dag{k}", rxa[k].at[pl.ds(1, 5 if TWO_LEVEL[k] else 7)])
    for group, like in sizes:
        pltpu.make_async_copy(like, like, ssem.at[groups[group]]).wait()


def local(forward_end, partner_end, potential, species_label, arm_length):
    full = pltpu.VMEM((2, ROWS, NYL, 2 * LANES), F32)
    dma = pltpu.SemaphoreType.DMA

    def v(*shape):
        return pltpu.VMEM(shape, F32)

    wide = 2 * LANES
    nh = [h[0][1] for h in HALF]
    return pl.pallas_call(
        kernel,
        name="star",
        out_shape=[jax.ShapeDtypeStruct(forward_end.shape, F32), jax.ShapeDtypeStruct(potential.shape, F32)],
        in_specs=[pl.BlockSpec(memory_space=pl.ANY)] * 4,
        out_specs=[pl.BlockSpec(memory_space=pltpu.VMEM)] * 2,
        scratch_shapes=[
            pltpu.SMEM((4,), jnp.int32), full, full, full, full,
            v(2, ROWS, 24, LANES), v(2, 10, 24, LANES), v(2, ROWS, 8, LANES), v(2, 10, 8, LANES),
            v(2, 10, 2, 2, 8, LANES),
            v(2, 10, 2, YD, LANES), v(2, 10, 2, YD, LANES), v(2, 10, 2, YD, LANES),
        ]
        + [v(ROWS, 2, n, LANES) for n in YC]
        + [v(8, n, LANES) for n in YC]
        + [v(2, n, LANES) for n in YC]
        + [v(10, 2, n, LANES) for n in YC]
        + [v(10, 2, 2, n, LANES) for n in YC]
        + [v(10, 2, 2, n, LANES) for n in YC]
        + [v(2, ROWS, 2 * n, wide) for n in nh]
        + [v(8, 2 * n, wide) for n in nh]
        + [dma((n,)) for n in (4, SEMS, SEMS)],
        compiler_params=pltpu.CompilerParams(collective_id=0, has_side_effects=True, vmem_limit_bytes=51 << 20),
        cost_estimate=pl.CostEstimate(flops=20_000_000, bytes_accessed=5 << 20, transcendentals=1 << 19),
    )(jnp.concatenate([species_label, arm_length]), forward_end, partner_end, potential)


def solution(mesh):
    return jax.shard_map(
        local,
        mesh=mesh,
        in_specs=(
            P("arm", "sx", "sy", None),
            P("arm", "sx", "sy", None),
            P(None, "sx", "sy", None),
            P("arm"),
            P("arm"),
        ),
        out_specs=(P("arm", "sx", "sy", None), P(None, "sx", "sy", None)),
        check_vma=False,
    )
```

```python
import jax
import jax.numpy as jnp
from jax import lax
from jax.experimental import pallas as pl
from jax.experimental.pallas import tpu as pltpu
from jax.sharding import PartitionSpec as P

MESH = pl.DeviceIdType.MESH
F32 = jnp.float32
ROWS, NYL, LANES = 4, 128, 128
YD, Y0 = 160, 16
BOUNDS = ((32, 96), (8, 120), (0, 128))
RESULT = ((40, 88), (16, 112), (0, 128))
NC = len(BOUNDS)
TWO_LEVEL = (True, True, False)
DIRECT_P = (True, False, True)


def segments(bounds, k):
    lo, hi = bounds[k]
    if k == 0:
        return ((0, lo, hi - lo),)
    lo_in, hi_in = bounds[k - 1]
    return ((0, hi_in, hi - hi_in), (hi - hi_in, lo, lo_in - lo))


SEG = [segments(BOUNDS, k) for k in range(NC)]
YC = [sum(n for _, _, n in s) for s in SEG]
_lo, _n = RESULT[0][0], (RESULT[0][1] - RESULT[0][0]) // 2
HALF = [((_lo, _n), (_lo + _n, _n))] + [tuple((s, n) for _, s, n in segments(RESULT, k)) for k in range(1, NC)]
TILES = [tuple(range(BOUNDS[0][0] // 8, BOUNDS[0][1] // 8))]
for _k in range(1, NC):
    _end = 1 if _k == NC - 1 else 0
    TILES.append(
        tuple(range(BOUNDS[_k - 1][1] // 8 - 1, BOUNDS[_k][1] // 8 + _end))
        + tuple(range(BOUNDS[_k][0] // 8 - _end, BOUNDS[_k - 1][0] // 8 + 1))
    )
SEMS = 7 * NC + 3 - sum(DIRECT_P) + sum(TWO_LEVEL)
PLACE = {}
for _k in range(NC):
    for _o, _s, _n in SEG[_k]:
        for _b in range(0, _n, 8):
            PLACE[(_s + _b) // 8] = (_k, _o + _b)


def lanes(h):
    return slice(h * LANES, (h + 1) * LANES)


def kernel(label_length, fwd, par, pot, conj, dens, *scratch):
    scratch = list(scratch)

    def take(n):
        out = scratch[:n]
        del scratch[:n]
        return out

    scalars, fv, pv, uv, ifac, es, ce, pes, pe, gp, v1, v2, v3 = take(13)
    p, prx, pxx, pf, g, q = (take(NC) for _ in range(6))
    da, rxa = (take(NC) for _ in range(2))
    lsem, ssem, rsem = take(3)

    arm, sx, sy = lax.axis_index("arm"), lax.axis_index("sx"), lax.axis_index("sy")
    x, y = arm // 4, arm % 4
    ox = 1 - x
    ys = [y, y + 1 - 2 * (y % 2), (y + 2) % 4, 3 - y]
    peers = [((x, ox)[d // 4], ys[d % 4]) for d in range(8)]
    up, down, other = (sx + 1) % 32, (sx + 31) % 32, 1 - sy

    def arm_dev(d):
        return {"arm": peers[d][0] * 4 + peers[d][1]}

    around = [{"sx": up}, {"sx": down}, {"sy": other}, {"sx": up, "sy": other}, {"sx": down, "sy": other}]

    quarters = [pl.ds(r, 1) for r in range(ROWS)]
    for r in quarters:
        pltpu.make_async_copy(fwd.at[:, r], fv.at[:, r], lsem.at[0]).start()
    for i, (src, dst) in enumerate(((pot, uv), (label_length, scalars), (par, pv))):
        pltpu.make_async_copy(src, dst, lsem.at[i + 1]).start()

    def loaded(i, src, dst):
        pltpu.make_async_copy(src, dst, lsem.at[i]).wait()

    groups = {}

    def send(group, src, dst, dev):
        n = groups.setdefault(group, len(groups))
        pltpu.make_async_remote_copy(
            src_ref=src, dst_ref=dst, send_sem=ssem.at[n], recv_sem=rsem.at[n], device_id=dev, device_id_type=MESH
        ).start()

    sizes = []

    def arrived(group, like):
        pltpu.make_async_copy(like, like, rsem.at[groups[group]]).wait()
        sizes.append((group, like))

    barrier = pltpu.get_barrier_semaphore()
    for d in range(1, 8):
        pl.semaphore_signal(barrier, inc=1, device_id=arm_dev(d), device_id_type=MESH)
    for dev in around:
        pl.semaphore_signal(barrier, inc=1, device_id=dev, device_id_type=MESH)

    loaded(0, fwd, fv)

    @pl.loop(0, ROWS)
    def _(r):
        for k in range(NC):
            for o, s, n in SEG[k]:
                for h in range(2):
                    p[k][r, h, o:o + n] = fv[0, r, s:s + n, lanes(h)] * fv[1, r, s:s + n, lanes(h)]

    def work_out(k):
        @pl.loop(0, ROWS)
        def _(r):
            for o, s, n in SEG[k]:
                for h in range(2):
                    for b in range(0, n, 8):
                        ya, oa = s + b, o + b
                        u0, u1 = (uv[i, r, ya:ya + 8, lanes(h)] for i in range(2))
                        for a in range(2):
                            e = jnp.exp(-0.5 * jnp.where(l[a], u1, u0))
                            ge = e / fv[a, r, ya:ya + 8, lanes(h)]
                            qe = (0.16 * e) * e
                            g[k][r + 3, a, h, oa:oa + 8] = ge
                            q[k][r + 3, a, h, oa:oa + 8] = qe
                            ifac[a, r, ya:ya + 8, lanes(h)] = 1.0 / e
                            i, j = a * 6 + h * 3, 12 + a * 4 + h * 2
                            if ya == 0:
                                es[0, r, i:i + 3] = ge[0:3]
                                es[0, r, j:j + 2] = qe[0:2]
                            if ya == NYL - 8:
                                es[1, r, i:i + 3] = ge[5:8]
                                es[1, r, j:j + 2] = qe[6:8]

    pl.semaphore_wait(barrier, 12)

    g_rows = ((pl.ds(4, 3), pl.ds(0, 3)), (pl.ds(3, 3), pl.ds(7, 3)))
    q_rows = ((pl.ds(5, 2), pl.ds(1, 2)), (pl.ds(3, 2), pl.ds(7, 2)))

    def edges(group, src, dst, corners):
        for side in range(2):
            send(group, src.at[side], dst.at[side, pl.ds(3, 4)], around[2])
            if corners:
                send(group, src.at[side, pl.ds(1, 3)], dst.at[side, pl.ds(0, 3)], around[3])
                send(group, src.at[side, pl.ds(0, 3)], dst.at[side, pl.ds(7, 3)], around[4])

    def forward_corners():
        arrived("edge", es)
        for side in range(2):
            send("corner", ce.at[side, pl.ds(4, 3)], ce.at[side, pl.ds(0, 3)], around[0])
            send("corner", ce.at[side, pl.ds(3, 3)], ce.at[side, pl.ds(7, 3)], around[1])

    def scatter(k):
        if DIRECT_P[k]:
            for d in range(1, 8):
                px, py = peers[d]
                send(f"rs{k}", p[k].at[py, px], prx[k].at[d], arm_dev(d))
        else:
            for d in (1, 2, 3):
                send(f"rs{k}", p[k].at[ys[d]], prx[k].at[pl.ds(2 * d, 2)], arm_dev(d))

    def coefficients(k):
        for i in range(2):
            send(f"coef{k}", g[k].at[g_rows[i][0]], g[k].at[g_rows[i][1]], around[i])
            send(f"coef{k}", q[k].at[q_rows[i][0]], q[k].at[q_rows[i][1]], around[i])

    def cross(k):
        if DIRECT_P[k]:
            return
        arrived(f"rs{k}", prx[k].at[pl.ds(2, 6)])
        for h in range(2):
            for b in range(0, YC[k], 16):
                c = slice(b, b + 16)
                prx[k][h, c] = (p[k][y, h, c] * prx[k][2 + h, c]) * (prx[k][4 + h, c] * prx[k][6 + h, c])
        send(f"xp{k}", prx[k].at[pl.ds(0, 2)], pxx[k], arm_dev(4))

    def gather(k):
        if DIRECT_P[k]:
            arrived(f"rs{k}", prx[k].at[pl.ds(1, 7)])
            for b in range(0, YC[k], 16):
                acc = p[k][y, x, b:b + 16]
                for d in range(1, 8):
                    acc = acc * prx[k][d, b:b + 16]
                pf[k][3 + y, x, b:b + 16] = acc
            mine = pf[k].at[3 + y, x]
            for d in range(1, 8):
                send(f"ag{k}", mine, mine, arm_dev(d))
        else:
            arrived(f"xp{k}", pxx[k])
            for h in range(2):
                for b in range(0, YC[k], 16):
                    pf[k][3 + y, h, b:b + 16] = prx[k][h, b:b + 16] * pxx[k][h, b:b + 16]
            mine = pf[k].at[3 + y]
            for d in (1, 2, 3):
                send(f"ag{k}", mine, mine, arm_dev(d))

    def product_halo(k):
        arrived(f"ag{k}", prx[k].at[pl.ds(1, 7) if DIRECT_P[k] else pl.ds(2, 6)])
        for i in range(2):
            send(f"ph{k}", pf[k].at[g_rows[i][0]], pf[k].at[g_rows[i][1]], around[i])
        if k == NC - 1:
            k0, o0 = PLACE[0]
            k1, o1 = PLACE[NYL // 8 - 1]
            for r in range(ROWS):
                for h in range(2):
                    pes[0, r, 3 * h:3 * h + 3] = pf[k0][r + 3, h, o0:o0 + 3]
                    pes[1, r, 3 * h:3 * h + 3] = pf[k1][r + 3, h, o1 + 5:o1 + 8]
            edges("pe", pes, pe, True)

    scatter(0)
    scatter(2)
    loaded(1, pot, uv)
    loaded(2, label_length, scalars)
    l = [scalars[a] == 1 for a in range(2)]
    work_out(0)
    coefficients(0)
    work_out(2)
    scatter(1)
    coefficients(2)
    edges("edge", es, ce, False)
    work_out(1)
    gather(0)
    gather(2)
    coefficients(1)
    cross(1)
    forward_corners()
    gather(1)
    product_halo(0)
    product_halo(2)
    product_halo(1)

    lane = lax.broadcasted_iota(jnp.int32, (8, LANES), 1)
    first, last = lane == 0, lane == LANES - 1

    def q_tile(a, r, h, t):
        if t in (-1, 16):
            return gp[0 if t == 16 else 1, r, a, h]
        k, o = PLACE[t]
        return q[k][r, a, h, o:o + 8]

    def advance(src, a, r, t, active):
        b = Y0 + 8 * t
        v = [src[a, r, h, b:b + 8] for h in range(2)]
        right = [pltpu.roll(w, 1, 1) for w in v]
        left = [pltpu.roll(w, LANES - 1, 1) for w in v]
        out = []
        for h in range(2):
            s = src[a, r - 1, h, b:b + 8] + src[a, r + 1, h, b:b + 8]
            s = s + (src[a, r, h, b - 1:b + 7] + src[a, r, h, b + 1:b + 9])
            s = s + (jnp.where(first, right[1 - h], right[h]) + jnp.where(last, left[1 - h], left[h]))
            new = q_tile(a, r, h, t) * (0.25 * v[h] + s)
            out.append(jnp.where(active, new, v[h]))
        return out

    def steps(k):
        arrived(f"coef{k}", g[k])
        arrived(f"ph{k}", pf[k].at[pl.ds(0, 6)])
        if k == NC - 1:
            arrived("corner", ce.at[:, pl.ds(0, 6)])
            arrived("pe", pe)

        @pl.loop(0, 10)
        def _(r):
            for o, s, n in SEG[k]:
                for h in range(2):
                    f = pf[k][r, h, o:o + n]
                    for a in range(2):
                        v1[a, r, h, Y0 + s:Y0 + s + n] = f * g[k][r, a, h, o:o + n]
            if k == NC - 1:
                for side, b in ((0, Y0 + NYL), (1, Y0 - 3)):
                    for h in range(2):
                        f = pe[side, r, 3 * h:3 * h + 3]
                        for a in range(2):
                            i, j = a * 6 + h * 3, 12 + a * 4 + h * 2
                            v1[a, r, h, b:b + 3] = f * ce[side, r, i:i + 3]
                            gp[side, r, a, h, 6 * side:6 * side + 2] = ce[side, r, j:j + 2]

        for t, (src, dst) in enumerate(((v1, v2), (v2, v3))):
            act = [scalars[2 + a] > t for a in range(2)]

            @pl.loop(1 + t, 9 - t, unroll=2)
            def _(r):
                for tile in TILES[k]:
                    b = Y0 + 8 * tile
                    for a in range(2):
                        out = advance(src, a, r, tile, act[a])
                        for h in range(2):
                            dst[a, r, h, b:b + 8] = out[h]

        act = [scalars[2 + a] > 2 for a in range(2)]
        for i in (1, 2, 3, 0):
            r = ys[i]
            for half in range(2):
                s0, n0 = HALF[k][half]
                for m in range(0, n0, 8):
                    b = s0 + m
                    w = []
                    for a in range(2):
                        out = advance(v3, a, r + 3, b // 8, act[a])
                        ws = []
                        for h in range(2):
                            c = out[h] * ifac[a, r, b:b + 8, lanes(h)]
                            conj[a, r, b:b + 8, lanes(h)] = c
                            ws.append(c * pv[a, r, b:b + 8, lanes(h)])
                        w.append(ws)
                    for h in range(2):
                        zero = jnp.where(l[0], 0.0, w[0][h]) + jnp.where(l[1], 0.0, w[1][h])
                        one = jnp.where(l[0], w[0][h], 0.0) + jnp.where(l[1], w[1][h], 0.0)
                        o = m + half * n0
                        da[k][0, r, o:o + 8, lanes(h)] = zero
                        da[k][1, r, o:o + 8, lanes(h)] = one
            for j in (i, i + 4):
                if j:
                    px, py = peers[j]
                    send(f"drs{k}", da[k].at[px, py], rxa[k].at[j], arm_dev(j))

    def gather_density(k):
        arrived(f"drs{k}", rxa[k].at[pl.ds(1, 7)])
        o = 0
        for s, n in HALF[k]:
            for h in range(2):
                for b in range(0, n, 8):
                    c = slice(o + b, o + b + 8)
                    acc = da[k][x, y, c, lanes(h)]
                    for d in range(1, 8):
                        acc = acc + rxa[k][d, c, lanes(h)]
                    dens[x, y, s + b:s + b + 8, lanes(h)] = acc
            o += n
        parts = [dens.at[x, y, pl.ds(s, n)] for s, n in HALF[k]]
        if TWO_LEVEL[k]:
            send(f"first{k}", parts[1], parts[1], arm_dev(4))
            for d in (1, 2, 3):
                send(f"first{k}", parts[0], parts[0], arm_dev(d))
            send(f"dag{k}", parts[0], parts[0], arm_dev(4))
            for d in (1, 2, 3):
                send(f"dag{k}", parts[1], parts[1], arm_dev(d))
        else:
            for piece in parts:
                for d in range(1, 8):
                    send(f"dag{k}", piece, piece, arm_dev(d))

    def pass_on(k):
        if TWO_LEVEL[k]:
            (s0, n0), (s1, n1) = HALF[k]
            arrived(f"first{k}", rxa[k].at[pl.ds(1, 2)])
            for d in (1, 2, 3):
                piece = dens.at[x, ys[d], pl.ds(s0, n0)]
                send(f"dag{k}", piece, piece, arm_dev(4))
            piece = dens.at[ox, y, pl.ds(s1, n1)]
            for d in (1, 2, 3):
                send(f"dag{k}", piece, piece, arm_dev(d))

    loaded(3, par, pv)
    for k in range(NC):
        steps(k)
    for k in range(NC):
        gather_density(k)
    for k in range(NC):
        pass_on(k)
    for k in range(NC):
        arrived(f"dag{k}", rxa[k].at[pl.ds(1, 5 if TWO_LEVEL[k] else 7)])
    for group, like in sizes:
        pltpu.make_async_copy(like, like, ssem.at[groups[group]]).wait()


def local(forward_end, partner_end, potential, species_label, arm_length):
    full = pltpu.VMEM((2, ROWS, NYL, 2 * LANES), F32)
    dma = pltpu.SemaphoreType.DMA

    def v(*shape):
        return pltpu.VMEM(shape, F32)

    wide = 2 * LANES
    nh = [h[0][1] for h in HALF]
    return pl.pallas_call(
        kernel,
        name="star",
        out_shape=[jax.ShapeDtypeStruct(forward_end.shape, F32), jax.ShapeDtypeStruct(potential.shape, F32)],
        in_specs=[pl.BlockSpec(memory_space=pl.ANY)] * 4,
        out_specs=[pl.BlockSpec(memory_space=pltpu.VMEM)] * 2,
        scratch_shapes=[
            pltpu.SMEM((4,), jnp.int32), full, full, full, full,
            v(2, ROWS, 24, LANES), v(2, 10, 24, LANES), v(2, ROWS, 8, LANES), v(2, 10, 8, LANES),
            v(2, 10, 2, 2, 8, LANES),
            v(2, 10, 2, YD, LANES), v(2, 10, 2, YD, LANES), v(2, 10, 2, YD, LANES),
        ]
        + [v(ROWS, 2, n, LANES) for n in YC]
        + [v(8, n, LANES) for n in YC]
        + [v(2, n, LANES) for n in YC]
        + [v(10, 2, n, LANES) for n in YC]
        + [v(10, 2, 2, n, LANES) for n in YC]
        + [v(10, 2, 2, n, LANES) for n in YC]
        + [v(2, ROWS, 2 * n, wide) for n in nh]
        + [v(8, 2 * n, wide) for n in nh]
        + [dma((n,)) for n in (4, SEMS, SEMS)],
        compiler_params=pltpu.CompilerParams(collective_id=0, has_side_effects=True, vmem_limit_bytes=51 << 20),
        cost_estimate=pl.CostEstimate(flops=20_000_000, bytes_accessed=5 << 20, transcendentals=1 << 19),
    )(jnp.concatenate([species_label, arm_length]), forward_end, partner_end, potential)


def solution(mesh):
    return jax.shard_map(
        local,
        mesh=mesh,
        in_specs=(
            P("arm", "sx", "sy", None),
            P("arm", "sx", "sy", None),
            P(None, "sx", "sy", None),
            P("arm"),
            P("arm"),
        ),
        out_specs=(P("arm", "sx", "sy", None), P(None, "sx", "sy", None)),
        check_vma=False,
    )
```
